256 devices in a mesh: dp: 256 (over y, z, x, core).
Axes of the slice: x: 4, y: 4, z: 8, core: 2. Of those that a mesh axis runs over, the one named last changes fastest.
Arguments:
- grads: bfloat16 [512, 1024, 1024], P('dp'), may hold values from -6 to 6
- memory: bfloat16 [512, 1024, 1024], P('dp'), may hold values from -6 to 6
- block_ids: int32 [16], replicated, may hold values from 0 to 63, as said below
- layer_ids: int32 [16], replicated, may hold values from 0 to 1, as said below
- master: float32 [128, 16384], P(None, 'dp'), may hold values from -8 to 8
- first_moment: float32 [128, 16384], P(None, 'dp'), may hold values from -8 to 8
- second_moment: float32 [128, 16384], P(None, 'dp'), may hold values from 0.25 to 4
Outputs:
- new_memory: bfloat16 [512, 1024, 1024], P('dp')
- master_new: float32 [128, 16384], P(None, 'dp')
- first_new: float32 [128, 16384], P(None, 'dp')
- second_new: float32 [128, 16384], P(None, 'dp')
- step_blocks: bfloat16 [16, 16384], replicated
The draws below stay inside these ranges and needn't reach their ends.
Inputs may be any that keep to these rules, and one draw needn't show every extreme that they name: Block ids number the 64 tiles of a layer, and the pairs (layer_ids[k], block_ids[k]) are distinct. `layer_ids`: every layer is named by at least a quarter of the 16 entries, rounded down.
All inputs are finite; a program needn't handle non-finite values.
Results may differ from the reference program's by a relative error of at most 0.0004.
Values may be sent and summed in bfloat16 or wider, within the bound.
No kernel may reach another device: no remote copies, remote signals or barrier semaphores. Data moves between devices by JAX's collectives and lax.ppermute only.
A program may use at most 64 MiB of HBM per device.

```python
import math
import jax
import jax.numpy as jnp
from jax import lax

D = 1024
LAYERS = 2
TILE = 128
SEL = 16
BLOCKS_LAYER = 64
BLOCKS = 128
TILE_ENT = 16384
N_DP = 256


def pick_entries(key):
    folded = jax.random.fold_in(key, 7)
    key_count, key_first, key_second, key_shuffle = jax.random.split(folded, 4)
    least = SEL // 4
    count_first = jax.random.randint(key_count, (), least, SEL - least + 1)
    first_perm = jax.random.permutation(key_first, BLOCKS_LAYER)[:SEL]
    second_perm = jax.random.permutation(key_second, BLOCKS_LAYER)[:SEL]
    position = jnp.arange(SEL, dtype=jnp.int32)
    layer_list = (position >= count_first).astype(jnp.int32)
    later_index = jnp.clip(position - count_first, 0, SEL - 1)
    block_list = jnp.where(layer_list == 0, first_perm[position], second_perm[later_index]).astype(jnp.int32)
    shuffle = jax.random.permutation(key_shuffle, SEL)
    return (layer_list[shuffle], block_list[shuffle])


def draw_block_ids(key, part):
    return pick_entries(key)[1]


def draw_layer_ids(key, part):
    return pick_entries(key)[0]


def rising_field(key):
    entry_row = (jnp.arange(TILE_ENT) // TILE).astype(jnp.float32)
    factor = 1.0 + 2.0 * entry_row / (TILE - 1)
    normal_part = jnp.clip(jax.random.normal(key, (BLOCKS, TILE_ENT), jnp.float32), -4.0, 4.0)
    return normal_part * factor[None, :] * 0.5


def draw_master(key, part):
    return rising_field(jax.random.fold_in(key, 11))


def draw_first_moment(key, part):
    return rising_field(jax.random.fold_in(key, 23))


def shard_levels(key, shape, shards, smallest, high):
    def one(axis_at, parts):
        heights = jax.random.uniform(jax.random.fold_in(jax.random.fold_in(key, 6), axis_at), (parts,), jnp.float32, smallest / len(shards), high / len(shards))
        return jnp.repeat(jnp.exp(heights), shape[axis_at] // parts).reshape((-1,) + (1,) * (len(shape) - axis_at - 1))

    gain = one(*shards[0])
    for cut in shards[1:]:
        gain = gain * one(*cut)
    return gain


def scatter_about(rng, extent, deviation, limit, cuts=(), kind=jnp.bfloat16):
    loudness = shard_levels(rng, extent, cuts, -0.22, 0.18) if cuts else 1.0
    entries = jax.random.normal(rng, extent, jnp.float32) * deviation * loudness
    return jnp.minimum(jnp.maximum(entries, -limit), limit).astype(kind)


def setup_inputs(seed: int = 0) -> dict:
    seeds = jax.random.split(jax.random.key(seed), 8)
    return {
        "grads": scatter_about(seeds[0], (N_DP * LAYERS, D, D), 0.5, 6.0, ((0, 256),)),
        "memory": scatter_about(seeds[1], (N_DP * LAYERS, D, D), 0.5, 6.0, ((0, 256),)),
        "block_ids": draw_block_ids(jax.random.fold_in(seeds[7], 71), 0),
        "layer_ids": draw_layer_ids(jax.random.fold_in(seeds[7], 71), 0),
        "master": draw_master(jax.random.fold_in(seeds[7], 71), 0),
        "first_moment": draw_first_moment(jax.random.fold_in(seeds[7], 71), 0),
        "second_moment": jnp.clip(jnp.exp(math.log(4.0) - 2.7725887 * jax.random.uniform(seeds[6], (BLOCKS, TILE_ENT), jnp.float32) ** shard_levels(seeds[6], (BLOCKS, TILE_ENT), ((1, 256),), -0.2, 0.2)), 0.25, 4.0),
    }


filter_rate = 0.3
beta_one = 0.9
beta_two = 0.999
adam_eps = 1e-06
weight_decay = 0.01
learn_rate = 0.01
norm_eps = 1e-06

def take_tiles(source, layer_ids, tile_row, tile_col):

    def single(layer_id, row_tile, col_tile):
        return lax.dynamic_slice(source, (layer_id, row_tile * TILE, col_tile * TILE), (1, TILE, TILE))[0]
    return jax.vmap(single)(layer_ids, tile_row, tile_col)

def pack_blocks(grads_dev, memory_dev, layer_ids, tile_row, tile_col):
    grad_tiles = take_tiles(grads_dev, layer_ids, tile_row, tile_col).astype(jnp.float32)
    memory_tiles = take_tiles(memory_dev, layer_ids, tile_row, tile_col).astype(jnp.float32)
    combined = grad_tiles + memory_tiles
    return combined.reshape(combined.shape[0], TILE * TILE)

def selected_mask(layer_ids, block_ids, layers, tile_count):
    columns = layer_ids * (tile_count * tile_count) + block_ids
    all_columns = jnp.arange(layers * tile_count * tile_count, dtype=jnp.int32)
    chosen = jnp.any(columns[:, None] == all_columns[None, :], axis=0)
    return chosen.reshape(layers, tile_count, 1, tile_count, 1)

def filter_memory(grads_dev, memory_dev, chosen):
    layers, model_width, _ = grads_dev.shape
    tile_count = model_width // TILE
    accumulated = grads_dev.astype(jnp.float32) + memory_dev.astype(jnp.float32)
    shaped = accumulated.reshape(layers, tile_count, TILE, tile_count, TILE)
    filtered = jnp.where(chosen, jnp.float32(0.0), shaped).reshape(layers, model_width, model_width)
    mixed = (1.0 - filter_rate) * memory_dev.astype(jnp.float32) + filter_rate * filtered
    return mixed.astype(jnp.bfloat16)

def adam_rows(summed, weights_sel, first_old, second_old):
    first_sel = beta_one * first_old + (1.0 - beta_one) * summed
    second_sel = beta_two * second_old + (1.0 - beta_two) * summed * summed
    update = first_sel / (jnp.sqrt(second_sel) + adam_eps) + weight_decay * weights_sel
    return (first_sel, second_sel, update)

def layer_squares(member, values):
    return lax.optimization_barrier(jnp.sum(member * lax.optimization_barrier(jnp.sum(values * values, axis=1))[:, None], axis=0))

def trust_rows(member, weight_total, update_total):
    trust_ratio = jnp.sqrt(weight_total / (update_total + norm_eps))
    return lax.optimization_barrier(jnp.sum(member * trust_ratio[None, :], axis=1))

def reference(grads, memory, block_ids, layer_ids, master, first_moment, second_moment):
    tile_count = D // TILE
    tile_row = block_ids // tile_count
    tile_col = block_ids % tile_count
    chosen = selected_mask(layer_ids, block_ids, LAYERS, tile_count)
    grads_view = grads.reshape(N_DP, LAYERS, D, D)
    memory_view = memory.reshape(N_DP, LAYERS, D, D)

    def per_device(running, arrays):
        grads_dev, memory_dev = arrays
        packed = pack_blocks(grads_dev, memory_dev, layer_ids, tile_row, tile_col)
        return (running + packed, filter_memory(grads_dev, memory_dev, chosen))
    summed, filtered_all = lax.scan(per_device, jnp.zeros((SEL, TILE * TILE), jnp.float32), (grads_view, memory_view))
    new_memory = filtered_all.reshape(N_DP * LAYERS, D, D)
    columns = layer_ids * BLOCKS_LAYER + block_ids
    weights_sel = jnp.take(master, columns, axis=0)
    first_old = jnp.take(first_moment, columns, axis=0)
    second_old = jnp.take(second_moment, columns, axis=0)
    first_sel, second_sel, update = adam_rows(summed, weights_sel, first_old, second_old)
    member = (layer_ids[:, None] == jnp.arange(LAYERS, dtype=jnp.int32)[None, :]).astype(jnp.float32)
    row_ratio = trust_rows(member, layer_squares(member, weights_sel), layer_squares(member, update))
    scaled = row_ratio[:, None] * update
    step_blocks = scaled.astype(jnp.bfloat16)
    master_new = master.at[columns].set(weights_sel - learn_rate * scaled)
    first_new = first_moment.at[columns].set(first_sel)
    second_new = second_moment.at[columns].set(second_sel)
    return (new_memory, master_new, first_new, second_new, step_blocks)
```

```python
import functools

import jax
import jax.numpy as jnp
from jax import lax
from jax.experimental import pallas as pl
from jax.experimental.pallas import tpu as pltpu
from jax.sharding import Mesh
from jax.sharding import PartitionSpec as P

TILE = 128
SEL = 16
HALF = 64
Y, Z, X, C = 4, 8, 4, 2
YX = Y * X
TILES_SIDE = 8
BLOCKS_LAYER = 64

filter_rate = 0.3
beta_one = 0.9
beta_two = 0.999
adam_eps = 1e-06
weight_decay = 0.01
learn_rate = 0.01
norm_eps = 1e-06

f32 = jnp.float32
VMEM = pl.BlockSpec(memory_space=pltpu.VMEM)
SMEM = pl.BlockSpec(memory_space=pltpu.SMEM)
HBM = pl.BlockSpec(memory_space=pl.ANY)


def iota(shape, dim):
    return lax.broadcasted_iota(jnp.int32, shape, dim)


def one_hot(block_ref, layer_ref):
    sub = iota((SEL, 128), 0)
    column = jnp.zeros((SEL, 128), jnp.int32)
    for k in range(SEL):
        column = jnp.where(sub == k, layer_ref[k] * BLOCKS_LAYER + block_ref[k], column)
    return (column == iota((SEL, 128), 1)).astype(f32)


def layer_tile(layer_ref):
    sub = iota((8, 128), 0)
    low = iota((8, 128), 1) < HALF
    layer = jnp.zeros((8, 128), jnp.int32)
    for k in range(8):
        layer = jnp.where(sub == k, jnp.where(low, layer_ref[k], layer_ref[k + 8]), layer)
    return layer


def select_entries(hot, state):
    picked = lax.dot_general(
        hot, state, (((1,), (1,)), ((), ())), precision=lax.Precision.HIGHEST, preferred_element_type=f32
    )
    return jnp.concatenate([picked[:8], picked[8:]], axis=1)


def spread_entries(hot, tile):
    rows = jnp.concatenate([tile[:, :HALF], tile[:, HALF:]], axis=0)
    return lax.dot_general(
        rows, hot, (((0,), (0,)), ((), ())), precision=lax.Precision.HIGHEST, preferred_element_type=f32
    )


def pack_kernel(block_ref, layer_ref, grads, memory, keep_ref, send_ref, g_buf, m_buf, k_tmp, s_tmp, g_sem, m_sem):
    copies = []
    for k in (j + 8 * h for j in range(8) for h in range(2)):
        layer = layer_ref[k]
        row = pl.multiple_of((block_ref[k] // TILES_SIDE) * TILE, TILE)
        col = pl.multiple_of((block_ref[k] % TILES_SIDE) * TILE, TILE)
        at = (layer, pl.ds(row, TILE), pl.ds(col, TILE))
        for src, buf, sem in ((grads, g_buf, g_sem), (memory, m_buf, m_sem)):
            copy = pltpu.make_async_copy(src.at[at], buf.at[k], sem.at[k])
            copy.start()
            copies.append(copy)
    core = lax.axis_index("c")
    low = iota((TILE, TILE), 1) < HALF
    first_core = core == 0
    for j in range(8):
        for copy in copies[4 * j : 4 * j + 4]:
            copy.wait()
        a = g_buf[j].astype(f32) + m_buf[j].astype(f32)
        b = g_buf[j + 8].astype(f32) + m_buf[j + 8].astype(f32)
        for_first = jnp.where(low, a, pltpu.roll(b, HALF, 1))
        for_second = jnp.where(low, pltpu.roll(a, HALF, 1), b)
        k_tmp[j] = jnp.where(first_core, for_first, for_second)
        s_tmp[j] = jnp.where(first_core, for_second, for_first)
        for y in range(Y):
            for x in range(X):
                at = pl.ds((y * X + x) * 64 + j * 8, 8)
                rows = pl.ds(y * Z * X + x, Z, stride=X)
                keep_ref[at, :] = k_tmp[j, rows, :]
                send_ref[at, :] = s_tmp[j, rows, :]


def pack(block_ids, layer_ids, grads, memory):
    shape = jax.ShapeDtypeStruct((1024, 128), f32)
    return pl.pallas_call(
        pack_kernel,
        out_shape=(shape, shape),
        in_specs=[SMEM, SMEM, HBM, HBM],
        out_specs=(VMEM, VMEM),
        scratch_shapes=[
            pltpu.VMEM((SEL, TILE, TILE), jnp.bfloat16),
            pltpu.VMEM((SEL, TILE, TILE), jnp.bfloat16),
            pltpu.VMEM((8, TILE, TILE), f32),
            pltpu.VMEM((8, TILE, TILE), f32),
            pltpu.SemaphoreType.DMA((SEL,)),
            pltpu.SemaphoreType.DMA((SEL,)),
        ],
        cost_estimate=pl.CostEstimate(flops=10**6, bytes_accessed=2 << 20, transcendentals=0),
        name="pack_tiles",
    )(block_ids, layer_ids, grads, memory)


ROWS = 256


def filter_kernel(layer, block_ref, layer_ref, g_ref, m_ref, *rest):
    out_ref = rest[-1]
    step = pl.program_id(0)
    tile = iota((8, 1024), 1) // TILE
    for i in range(ROWS // TILE):
        first = (layer * TILES_SIDE + step * (ROWS // TILE) + i) * TILES_SIDE
        column = tile + first
        chosen = jnp.zeros((8, 1024), jnp.bool_)
        for k in range(SEL):
            chosen = jnp.logical_or(chosen, column == layer_ref[k] * BLOCKS_LAYER + block_ref[k])
        scale = jnp.where(chosen, f32(0.0), f32(1.0))[:1]
        for half in range(2):
            at = pl.ds(i * TILE + half * 64, 64)
            mem = m_ref[0, at, :].astype(f32)
            total = g_ref[0, at, :].astype(f32) + mem
            kept = jnp.where(scale > 0.5, total, f32(0.0))
            mixed = f32(1.0 - filter_rate) * mem + f32(filter_rate) * kept
            out_ref[0, at, :] = mixed.astype(jnp.bfloat16)


def filter_layer(layer, block_ids, layer_ids, grads, memory, into=None):
    spec = pl.BlockSpec((1, ROWS, 1024), lambda i, *_: (layer, i, 0))
    args = [block_ids, layer_ids, grads, memory]
    in_specs = [spec, spec]
    aliases = {}
    if into is not None:
        args.append(into)
        in_specs.append(HBM)
        aliases = {4: 0}
    return pl.pallas_call(
        functools.partial(filter_kernel, layer),
        out_shape=jax.ShapeDtypeStruct((2, 1024, 1024), jnp.bfloat16),
        grid_spec=pltpu.PrefetchScalarGridSpec(
            num_scalar_prefetch=2, grid=(1024 // ROWS,), in_specs=in_specs, out_specs=spec
        ),
        input_output_aliases=aliases,
        cost_estimate=pl.CostEstimate(flops=4 << 20, bytes_accessed=6 << 20, transcendentals=0),
        name="filter_memory",
    )(*args)


def moments_kernel(block_ref, layer_ref, master, first, second, out_ref):
    hot = one_hot(block_ref, layer_ref)
    for i, state in enumerate((first, second, master)):
        out_ref[pl.ds(8 * i, 8), :] = select_entries(hot, state[...])


def moments(block_ids, layer_ids, master, first, second):
    return pl.pallas_call(
        moments_kernel,
        out_shape=jax.ShapeDtypeStruct((24, 128), f32),
        in_specs=[SMEM, SMEM, VMEM, VMEM, VMEM],
        out_specs=VMEM,
        name="select_moments",
    )(block_ids, layer_ids, master, first, second)


def partial_kernel(got, own, out_ref, tmp):
    for j in range(8):
        total = got[0, pl.ds(8 * j, 8), :]
        for s in range(1, YX):
            total = total + got[s, pl.ds(8 * j, 8), :]
        tmp[pl.ds(j, Z, stride=8), :] = total
    for z in range(Z):
        out_ref[z, pl.ds(0, 64), :] = tmp[...]
        out_ref[z, pl.ds(64, 24), :] = own[...]


def partial_sums(got, own):
    return pl.pallas_call(
        partial_kernel,
        out_shape=jax.ShapeDtypeStruct((Z, 88, 128), f32),
        in_specs=[VMEM, VMEM],
        out_specs=VMEM,
        scratch_shapes=[pltpu.VMEM((64, 128), f32)],
        name="sum_partials",
    )(got, own)


def update_kernel(got, out_ref, own_sum, own_update):
    me = lax.axis_index("z")
    squares = jnp.zeros((8, 128), f32)
    for z in range(Z):
        at = pl.ds(8 * z, 8)
        summed = got[0, at, :]
        for s in range(1, Z):
            summed = summed + got[s, at, :]
        first = got[z, pl.ds(64, 8), :]
        second = got[z, pl.ds(72, 8), :]
        weights = got[z, pl.ds(80, 8), :]
        first_sel = beta_one * first + (1.0 - beta_one) * summed
        second_sel = beta_two * second + (1.0 - beta_two) * summed * summed
        update = first_sel / (jnp.sqrt(second_sel) + adam_eps) + weight_decay * weights
        squares = squares + weights * weights
        for s in range(YX):
            out_ref[s, at, :] = update

        @pl.when(me == z)
        def _():
            own_sum[...] = summed
            own_update[...] = update

    for s in range(YX):
        out_ref[s, pl.ds(64, 8), :] = squares


def updates(got):
    tile = jax.ShapeDtypeStruct((8, 128), f32)
    return pl.pallas_call(
        update_kernel,
        out_shape=(jax.ShapeDtypeStruct((YX, 72, 128), f32), tile, tile),
        in_specs=[VMEM],
        out_specs=(VMEM, VMEM, VMEM),
        name="lamb_update",
    )(got)


def state_kernel(block_ref, layer_ref, own_sum, first, second, first_new, second_new):
    hot = one_hot(block_ref, layer_ref)
    named = jnp.max(hot, axis=0, keepdims=True) > 0.5
    summed = spread_entries(hot, own_sum[...])
    old = first[...]
    first_new[...] = jnp.where(named, beta_one * old + (1.0 - beta_one) * summed, old)
    old = second[...]
    second_new[...] = jnp.where(named, beta_two * old + (1.0 - beta_two) * summed * summed, old)


def new_moments(block_ids, layer_ids, own_sum, first, second):
    state = jax.ShapeDtypeStruct((HALF, 128), f32)
    return pl.pallas_call(
        state_kernel,
        out_shape=(state, state),
        in_specs=[SMEM, SMEM, VMEM, VMEM, VMEM],
        out_specs=(VMEM, VMEM),
        name="new_moments",
    )(block_ids, layer_ids, own_sum, first, second)


def step_kernel(block_ref, layer_ref, own, other, own_update, master, step_ref, master_new):
    update_sq = jnp.zeros((8, 128), f32)
    weight_sq = jnp.zeros((8, 128), f32)
    for ref in (own, other):
        for s in range(YX):
            for z in range(Z):
                value = ref[s, pl.ds(8 * z, 8), :]
                update_sq = update_sq + value * value
            weight_sq = weight_sq + ref[s, pl.ds(64, 8), :]
    layer = layer_tile(layer_ref)
    ratio = jnp.zeros((8, 128), f32)
    for which in range(2):
        mine = layer == which
        weight_total = jnp.sum(jnp.where(mine, weight_sq, 0.0), keepdims=True)
        update_total = jnp.sum(jnp.where(mine, update_sq, 0.0), keepdims=True)
        ratio = jnp.where(mine, jnp.sqrt(weight_total / (update_total + norm_eps)), ratio)
    low = iota((8, 128), 1) < HALF

    def write(left, right):
        for y in range(Y):
            for x in range(X):
                for z in range(Z):
                    at = (y * X + x, pl.ds(8 * z, 8))
                    a = ratio * left[at]
                    b = ratio * right[at]
                    top = jnp.where(low, a, pltpu.roll(b, HALF, 1))
                    bottom = jnp.where(low, pltpu.roll(a, HALF, 1), b)
                    row = (y * Z + z) * X + x
                    step_ref[:, pl.ds(row * TILE, TILE)] = jnp.concatenate([top, bottom], axis=0).astype(
                        jnp.bfloat16
                    )

    core = lax.axis_index("c")
    pl.when(core == 0)(lambda: write(own, other))
    pl.when(core == 1)(lambda: write(other, own))
    hot = one_hot(block_ref, layer_ref)
    named = jnp.max(hot, axis=0, keepdims=True) > 0.5
    scaled = spread_entries(hot, ratio * own_update[...])
    old = master[...]
    master_new[...] = jnp.where(named, old - learn_rate * scaled, old)


def steps(block_ids, layer_ids, own, other, own_update, master):
    return pl.pallas_call(
        step_kernel,
        out_shape=(
            jax.ShapeDtypeStruct((SEL, TILE * TILE), jnp.bfloat16),
            jax.ShapeDtypeStruct((HALF, 128), f32),
        ),
        in_specs=[SMEM, SMEM, VMEM, VMEM, VMEM, VMEM],
        out_specs=(VMEM, VMEM),
        name="scaled_step",
    )(block_ids, layer_ids, own, other, own_update, master)


def on_device(grads, memory, block_ids, layer_ids, master, first_moment, second_moment):
    swap = [(0, 1), (1, 0)]
    master, first, second = master.T, first_moment.T, second_moment.T
    keep, send = pack(block_ids, layer_ids, grads, memory)
    received = lax.ppermute(send, "c", swap)
    new_memory = filter_layer(0, block_ids, layer_ids, grads, memory)
    own = moments(block_ids, layer_ids, master, first, second)
    part = (keep + received).reshape(YX, 64, 128)
    got = lax.all_to_all(part, ("y", "x"), 0, 0, tiled=True)
    got = lax.all_to_all(partial_sums(got, own), "z", 0, 0, tiled=True)
    payload, own_sum, own_update = updates(got)
    mine = lax.all_to_all(payload, ("y", "x"), 0, 0, tiled=True)
    other = lax.ppermute(mine, "c", swap)
    new_memory = filter_layer(1, block_ids, layer_ids, grads, memory, new_memory)
    first_new, second_new = new_moments(block_ids, layer_ids, own_sum, first, second)
    step_blocks, master_new = steps(block_ids, layer_ids, mine, other, own_update, master)
    return (new_memory, master_new.T, first_new.T, second_new.T, step_blocks)


def solution(mesh):
    torus = Mesh(mesh.devices.reshape(Y, Z, X, C), ("y", "z", "x", "c"))
    dp = ("y", "z", "x", "c")
    replica = P(dp, None, None)
    state = P(None, dp)
    return jax.shard_map(
        on_device,
        mesh=torus,
        in_specs=(replica, replica, P(), P(), state, state, state),
        out_specs=(replica, state, state, state, P()),
        check_vma=False,
    )
```

```python
import functools

import jax
import jax.numpy as jnp
from jax import lax
from jax.experimental import pallas as pl
from jax.experimental.pallas import tpu as pltpu
from jax.sharding import Mesh
from jax.sharding import PartitionSpec as P

TILE = 128
SEL = 16
HALF = 64
Y, Z, X, C = 4, 8, 4, 2
YX = Y * X
TILES_SIDE = 8
BLOCKS_LAYER = 64

filter_rate = 0.3
beta_one = 0.9
beta_two = 0.999
adam_eps = 1e-06
weight_decay = 0.01
learn_rate = 0.01
norm_eps = 1e-06

f32 = jnp.float32
VMEM = pl.BlockSpec(memory_space=pltpu.VMEM)
SMEM = pl.BlockSpec(memory_space=pltpu.SMEM)
HBM = pl.BlockSpec(memory_space=pl.ANY)
LARGE = pltpu.CompilerParams(vmem_limit_bytes=16 << 20)
SMALL = pltpu.CompilerParams(vmem_limit_bytes=8 << 20)


def in_hbm(array):
    return pltpu.with_memory_space_constraint(array, pltpu.HBM)


def iota(shape, dim):
    return lax.broadcasted_iota(jnp.int32, shape, dim)


def one_hot(block_ref, layer_ref):
    sub = iota((SEL, 128), 0)
    column = jnp.zeros((SEL, 128), jnp.int32)
    for k in range(SEL):
        column = jnp.where(sub == k, layer_ref[k] * BLOCKS_LAYER + block_ref[k], column)
    return (column == iota((SEL, 128), 1)).astype(f32)


def layer_tile(layer_ref):
    sub = iota((8, 128), 0)
    low = iota((8, 128), 1) < HALF
    layer = jnp.zeros((8, 128), jnp.int32)
    for k in range(8):
        layer = jnp.where(sub == k, jnp.where(low, layer_ref[k], layer_ref[k + 8]), layer)
    return layer


def select_entries(hot, state):
    picked = lax.dot_general(
        hot, state, (((1,), (1,)), ((), ())), precision=lax.Precision.HIGHEST, preferred_element_type=f32
    )
    return jnp.concatenate([picked[:8], picked[8:]], axis=1)


def spread_entries(hot, tile):
    rows = jnp.concatenate([tile[:, :HALF], tile[:, HALF:]], axis=0)
    return lax.dot_general(
        rows, hot, (((0,), (0,)), ((), ())), precision=lax.Precision.HIGHEST, preferred_element_type=f32
    )


def pack_kernel(block_ref, layer_ref, grads, memory, keep_ref, send_ref, g_buf, m_buf, k_tmp, s_tmp, g_sem, m_sem):
    copies = []
    for k in (j + 8 * h for j in range(8) for h in range(2)):
        layer = layer_ref[k]
        row = pl.multiple_of((block_ref[k] // TILES_SIDE) * TILE, TILE)
        col = pl.multiple_of((block_ref[k] % TILES_SIDE) * TILE, TILE)
        at = (layer, pl.ds(row, TILE), pl.ds(col, TILE))
        for src, buf, sem in ((grads, g_buf, g_sem), (memory, m_buf, m_sem)):
            copy = pltpu.make_async_copy(src.at[at], buf.at[k], sem.at[k])
            copy.start()
            copies.append(copy)
    core = lax.axis_index("c")
    low = iota((TILE, TILE), 1) < HALF
    first_core = core == 0
    for j in range(8):
        for copy in copies[4 * j : 4 * j + 4]:
            copy.wait()
        a = g_buf[j].astype(f32) + m_buf[j].astype(f32)
        b = g_buf[j + 8].astype(f32) + m_buf[j + 8].astype(f32)
        for_first = jnp.where(low, a, pltpu.roll(b, HALF, 1))
        for_second = jnp.where(low, pltpu.roll(a, HALF, 1), b)
        k_tmp[j] = jnp.where(first_core, for_first, for_second)
        s_tmp[j] = jnp.where(first_core, for_second, for_first)
        for y in range(Y):
            for x in range(X):
                at = pl.ds((y * X + x) * 64 + j * 8, 8)
                rows = pl.ds(y * Z * X + x, Z, stride=X)
                keep_ref[at, :] = k_tmp[j, rows, :]
                send_ref[at, :] = s_tmp[j, rows, :]


def pack(block_ids, layer_ids, grads, memory):
    shape = jax.ShapeDtypeStruct((1024, 128), f32)
    return pl.pallas_call(
        pack_kernel,
        out_shape=(shape, shape),
        in_specs=[SMEM, SMEM, HBM, HBM],
        out_specs=(VMEM, VMEM),
        scratch_shapes=[
            pltpu.VMEM((SEL, TILE, TILE), jnp.bfloat16),
            pltpu.VMEM((SEL, TILE, TILE), jnp.bfloat16),
            pltpu.VMEM((8, TILE, TILE), f32),
            pltpu.VMEM((8, TILE, TILE), f32),
            pltpu.SemaphoreType.DMA((SEL,)),
            pltpu.SemaphoreType.DMA((SEL,)),
        ],
        cost_estimate=pl.CostEstimate(flops=10**6, bytes_accessed=2 << 20, transcendentals=0),
        compiler_params=SMALL,
        name="pack_tiles",
    )(block_ids, layer_ids, in_hbm(grads), in_hbm(memory))


PARTS = 8
ROWS = 2 * 1024 // PARTS
CHUNK = 16


def filter_kernel(
    block_ref, layer_ref, grads, memory, after, master, first, second, out, own, g_buf, m_buf, o_buf, g_sem, m_sem, o_sem
):
    def rows(part):
        return pl.ds(pl.multiple_of(part * ROWS, ROWS), ROWS)

    def read(part, src, buf, sem):
        return pltpu.make_async_copy(src.at[rows(part)], buf.at[rows(part)], sem.at[part])

    def write(part):
        return pltpu.make_async_copy(o_buf.at[rows(part)], out.at[rows(part)], o_sem.at[part])

    @pl.loop(0, PARTS)
    def _(part):
        read(part, grads, g_buf, g_sem).start()
        read(part, memory, m_buf, m_sem).start()

    hot = one_hot(block_ref, layer_ref)
    for i, state in enumerate((first, second, master)):
        own[pl.ds(8 * i, 8), :] = select_entries(hot, state[...])
    tile = iota((8, 1024), 1) // TILE

    @pl.loop(0, PARTS)
    def _(part):
        read(part, grads, g_buf, g_sem).wait()
        read(part, memory, m_buf, m_sem).wait()
        for i in range(ROWS // TILE):
            column = tile + (part * (ROWS // TILE) + i) * TILES_SIDE
            chosen = jnp.zeros((8, 1024), jnp.bool_)
            for k in range(SEL):
                chosen = jnp.logical_or(chosen, column == layer_ref[k] * BLOCKS_LAYER + block_ref[k])
            rate = jnp.where(chosen, f32(0.0), f32(filter_rate))
            rate = jnp.concatenate([rate] * (CHUNK // 8), axis=0)

            @pl.loop(0, TILE // CHUNK, unroll=TILE // CHUNK)
            def _(c):
                at = pl.ds(pl.multiple_of(part * ROWS + i * TILE + c * CHUNK, CHUNK), CHUNK)
                mem = m_buf[at, :].astype(f32)
                total = g_buf[at, :].astype(f32) + mem
                mixed = f32(1.0 - filter_rate) * mem + rate * total
                o_buf[at, :] = mixed.astype(jnp.bfloat16)

        write(part).start()

    @pl.loop(0, PARTS)
    def _(part):
        write(part).wait()


def filter_memory(block_ids, layer_ids, grads, memory, after, master, first, second):
    flat = (2 * 1024, 1024)
    buf = pltpu.VMEM(flat, jnp.bfloat16)
    sem = pltpu.SemaphoreType.DMA((PARTS,))
    out, own = pl.pallas_call(
        filter_kernel,
        out_shape=(jax.ShapeDtypeStruct(flat, jnp.bfloat16), jax.ShapeDtypeStruct((24, 128), f32)),
        in_specs=[SMEM, SMEM, HBM, HBM, HBM, VMEM, VMEM, VMEM],
        out_specs=(HBM, VMEM),
        scratch_shapes=[buf, buf, buf, sem, sem, sem],
        compiler_params=LARGE,
        cost_estimate=pl.CostEstimate(flops=8 << 20, bytes_accessed=12 << 20, transcendentals=0),
        name="filter_memory",
    )(block_ids, layer_ids, in_hbm(grads.reshape(flat)), in_hbm(memory.reshape(flat)), after, master, first, second)
    return out.reshape(2, 1024, 1024), own


def partial_kernel(got, own, out_ref, tmp):
    for j in range(8):
        total = got[0, pl.ds(8 * j, 8), :]
        for s in range(1, YX):
            total = total + got[s, pl.ds(8 * j, 8), :]
        tmp[pl.ds(j, Z, stride=8), :] = total
    for z in range(Z):
        out_ref[z, pl.ds(0, 64), :] = tmp[...]
        out_ref[z, pl.ds(64, 24), :] = own[...]


def partial_sums(got, own):
    return pl.pallas_call(
        partial_kernel,
        out_shape=jax.ShapeDtypeStruct((Z, 88, 128), f32),
        in_specs=[VMEM, VMEM],
        out_specs=VMEM,
        scratch_shapes=[pltpu.VMEM((64, 128), f32)],
        compiler_params=SMALL,
        name="sum_partials",
    )(got, own)


def update_kernel(got, out_ref, own_sum, own_update):
    me = lax.axis_index("z")
    squares = jnp.zeros((8, 128), f32)
    for z in range(Z):
        at = pl.ds(8 * z, 8)
        summed = got[0, at, :]
        for s in range(1, Z):
            summed = summed + got[s, at, :]
        first = got[z, pl.ds(64, 8), :]
        second = got[z, pl.ds(72, 8), :]
        weights = got[z, pl.ds(80, 8), :]
        first_sel = beta_one * first + (1.0 - beta_one) * summed
        second_sel = beta_two * second + (1.0 - beta_two) * summed * summed
        update = first_sel / (jnp.sqrt(second_sel) + adam_eps) + weight_decay * weights
        squares = squares + weights * weights
        for s in range(YX):
            out_ref[s, at, :] = update

        @pl.when(me == z)
        def _():
            own_sum[...] = summed
            own_update[...] = update

    for s in range(YX):
        out_ref[s, pl.ds(64, 8), :] = squares


def updates(got):
    tile = jax.ShapeDtypeStruct((8, 128), f32)
    return pl.pallas_call(
        update_kernel,
        out_shape=(jax.ShapeDtypeStruct((YX, 72, 128), f32), tile, tile),
        in_specs=[VMEM],
        out_specs=(VMEM, VMEM, VMEM),
        compiler_params=SMALL,
        name="lamb_update",
    )(got)


def state_kernel(block_ref, layer_ref, own_sum, first, second, first_new, second_new):
    hot = one_hot(block_ref, layer_ref)
    named = jnp.max(hot, axis=0, keepdims=True) > 0.5
    summed = spread_entries(hot, own_sum[...])
    old = first[...]
    first_new[...] = jnp.where(named, beta_one * old + (1.0 - beta_one) * summed, old)
    old = second[...]
    second_new[...] = jnp.where(named, beta_two * old + (1.0 - beta_two) * summed * summed, old)


def new_moments(block_ids, layer_ids, own_sum, first, second):
    state = jax.ShapeDtypeStruct((HALF, 128), f32)
    return pl.pallas_call(
        state_kernel,
        out_shape=(state, state),
        in_specs=[SMEM, SMEM, VMEM, VMEM, VMEM],
        out_specs=(VMEM, VMEM),
        compiler_params=SMALL,
        name="new_moments",
    )(block_ids, layer_ids, own_sum, first, second)


def step_kernel(block_ref, layer_ref, own, other, own_update, master, step_ref, master_new):
    update_sq = jnp.zeros((8, 128), f32)
    weight_sq = jnp.zeros((8, 128), f32)
    for ref in (own, other):
        for s in range(YX):
            for z in range(Z):
                value = ref[s, pl.ds(8 * z, 8), :]
                update_sq = update_sq + value * value
            weight_sq = weight_sq + ref[s, pl.ds(64, 8), :]
    layer = layer_tile(layer_ref)
    ratio = jnp.zeros((8, 128), f32)
    for which in range(2):
        mine = layer == which
        weight_total = jnp.sum(jnp.where(mine, weight_sq, 0.0), keepdims=True)
        update_total = jnp.sum(jnp.where(mine, update_sq, 0.0), keepdims=True)
        ratio = jnp.where(mine, jnp.sqrt(weight_total / (update_total + norm_eps)), ratio)
    low = iota((8, 128), 1) < HALF

    def write(left, right):
        for y in range(Y):
            for x in range(X):
                for z in range(Z):
                    at = (y * X + x, pl.ds(8 * z, 8))
                    a = ratio * left[at]
                    b = ratio * right[at]
                    top = jnp.where(low, a, pltpu.roll(b, HALF, 1))
                    bottom = jnp.where(low, pltpu.roll(a, HALF, 1), b)
                    row = (y * Z + z) * X + x
                    step_ref[:, pl.ds(row * TILE, TILE)] = jnp.concatenate([top, bottom], axis=0).astype(
                        jnp.bfloat16
                    )

    core = lax.axis_index("c")
    pl.when(core == 0)(lambda: write(own, other))
    pl.when(core == 1)(lambda: write(other, own))
    hot = one_hot(block_ref, layer_ref)
    named = jnp.max(hot, axis=0, keepdims=True) > 0.5
    scaled = spread_entries(hot, ratio * own_update[...])
    old = master[...]
    master_new[...] = jnp.where(named, old - learn_rate * scaled, old)


def steps(block_ids, layer_ids, own, other, own_update, master):
    return pl.pallas_call(
        step_kernel,
        out_shape=(
            jax.ShapeDtypeStruct((SEL, TILE * TILE), jnp.bfloat16),
            jax.ShapeDtypeStruct((HALF, 128), f32),
        ),
        in_specs=[SMEM, SMEM, VMEM, VMEM, VMEM, VMEM],
        out_specs=(VMEM, VMEM),
        compiler_params=SMALL,
        name="scaled_step",
    )(block_ids, layer_ids, own, other, own_update, master)


def on_device(grads, memory, block_ids, layer_ids, master, first_moment, second_moment):
    swap = [(0, 1), (1, 0)]
    block_ids, layer_ids = in_hbm(block_ids), in_hbm(layer_ids)
    master, first, second = master.T, first_moment.T, second_moment.T
    keep, send = pack(block_ids, layer_ids, grads, memory)
    received = lax.ppermute(send, "c", swap)
    part = (keep + received).reshape(YX, 64, 128)
    new_memory, own = filter_memory(block_ids, layer_ids, grads, memory, part, master, first, second)
    got = lax.all_to_all(part, ("y", "x"), 0, 0, tiled=True)
    sums = partial_sums(got, own)
    got = lax.all_to_all(sums, "z", 0, 0, tiled=True)
    payload, own_sum, own_update = updates(got)
    mine = lax.all_to_all(payload, ("y", "x"), 0, 0, tiled=True)
    other = lax.ppermute(mine, "c", swap)
    first_new, second_new = new_moments(block_ids, layer_ids, own_sum, first, second)
    step_blocks, master_new = steps(block_ids, layer_ids, mine, other, own_update, master)
    return (new_memory, master_new.T, first_new.T, second_new.T, step_blocks)


def solution(mesh):
    torus = Mesh(mesh.devices.reshape(Y, Z, X, C), ("y", "z", "x", "c"))
    dp = ("y", "z", "x", "c")
    replica = P(dp, None, None)
    state = P(None, dp)
    return jax.shard_map(
        on_device,
        mesh=torus,
        in_specs=(replica, replica, P(), P(), state, state, state),
        out_specs=(replica, state, state, state, P()),
        check_vma=False,
    )
```

```python
import functools

import jax
import jax.numpy as jnp
from jax import lax
from jax.experimental import pallas as pl
from jax.experimental.pallas import tpu as pltpu
from jax.sharding import Mesh
from jax.sharding import PartitionSpec as P

TILE = 128
SEL = 16
HALF = 64
Y, Z, X, C = 4, 8, 4, 2
YX = Y * X
TILES_SIDE = 8
BLOCKS_LAYER = 64

filter_rate = 0.3
beta_one = 0.9
beta_two = 0.999
adam_eps = 1e-06
weight_decay = 0.01
learn_rate = 0.01
norm_eps = 1e-06

f32 = jnp.float32
VMEM = pl.BlockSpec(memory_space=pltpu.VMEM)
SMEM = pl.BlockSpec(memory_space=pltpu.SMEM)
HBM = pl.BlockSpec(memory_space=pl.ANY)
LARGE = pltpu.CompilerParams(vmem_limit_bytes=16 << 20)
SMALL = pltpu.CompilerParams(vmem_limit_bytes=8 << 20)


def in_hbm(array):
    return pltpu.with_memory_space_constraint(array, pltpu.HBM)


def iota(shape, dim):
    return lax.broadcasted_iota(jnp.int32, shape, dim)


def one_hot(block_ref, layer_ref):
    sub = iota((SEL, 128), 0)
    column = jnp.zeros((SEL, 128), jnp.int32)
    for k in range(SEL):
        column = jnp.where(sub == k, layer_ref[k] * BLOCKS_LAYER + block_ref[k], column)
    return (column == iota((SEL, 128), 1)).astype(f32)


def layer_tile(layer_ref):
    sub = iota((8, 128), 0)
    low = iota((8, 128), 1) < HALF
    layer = jnp.zeros((8, 128), jnp.int32)
    for k in range(8):
        layer = jnp.where(sub == k, jnp.where(low, layer_ref[k], layer_ref[k + 8]), layer)
    return layer


def select_entries(hot, state):
    picked = lax.dot_general(
        hot, state, (((1,), (1,)), ((), ())), precision=lax.Precision.HIGHEST, preferred_element_type=f32
    )
    return jnp.concatenate([picked[:8], picked[8:]], axis=1)


def spread_entries(hot, tile):
    rows = jnp.concatenate([tile[:, :HALF], tile[:, HALF:]], axis=0)
    return lax.dot_general(
        rows, hot, (((0,), (0,)), ((), ())), precision=lax.Precision.HIGHEST, preferred_element_type=f32
    )


def half_columns(g_tiles, m_tiles, j, left):
    low = iota((TILE, TILE), 1) < HALF
    a = g_tiles[j].astype(f32) + m_tiles[j].astype(f32)
    b = g_tiles[j + 8].astype(f32) + m_tiles[j + 8].astype(f32)
    turned = pltpu.roll(jnp.where(left, b, a), HALF, 1)
    return jnp.where(low, jnp.where(left, a, turned), jnp.where(left, turned, b))


def store_rows(out_ref, tmp, j, value):
    tmp[j] = value
    for y in range(Y):
        for x in range(X):
            out_ref[pl.ds((y * X + x) * 64 + j * 8, 8), :] = tmp[j, pl.ds(y * Z * X + x, Z, stride=X), :]


def send_kernel(block_ref, layer_ref, grads, memory, send_ref, g_tiles, m_tiles, tmp, g_sem, m_sem):
    copies = []
    for k in (j + 8 * h for j in range(8) for h in range(2)):
        layer = layer_ref[k]
        row = pl.multiple_of((block_ref[k] // TILES_SIDE) * TILE, TILE)
        col = pl.multiple_of((block_ref[k] % TILES_SIDE) * TILE, TILE)
        at = (layer, pl.ds(row, TILE), pl.ds(col, TILE))
        for src, buf, sem in ((grads, g_tiles, g_sem), (memory, m_tiles, m_sem)):
            copy = pltpu.make_async_copy(src.at[at], buf.at[k], sem.at[k])
            copy.start()
            copies.append(copy)
    for j in range(8):
        for copy in copies[4 * j : 4 * j + 4]:
            copy.wait()
        store_rows(send_ref, tmp, j, half_columns(g_tiles, m_tiles, j, lax.axis_index("c") == 1))


def keep_kernel(block_ref, layer_ref, g_tiles, m_tiles, master, first, second, keep_ref, own_ref, hot_ref, layers_ref, tmp):
    for j in range(8):
        store_rows(keep_ref, tmp, j, half_columns(g_tiles, m_tiles, j, lax.axis_index("c") == 0))
    hot = one_hot(block_ref, layer_ref)
    hot_ref[...] = hot
    layers_ref[...] = layer_tile(layer_ref)
    for i, state in enumerate((first, second, master)):
        own_ref[pl.ds(8 * i, 8), :] = select_entries(hot, state[...])


def pack_send(block_ids, layer_ids, grads, memory):
    tiles = jax.ShapeDtypeStruct((SEL, TILE, TILE), jnp.bfloat16)
    return pl.pallas_call(
        send_kernel,
        out_shape=(jax.ShapeDtypeStruct((1024, 128), f32), tiles, tiles),
        in_specs=[SMEM, SMEM, HBM, HBM],
        out_specs=(VMEM, VMEM, VMEM),
        scratch_shapes=[
            pltpu.VMEM((8, TILE, TILE), f32),
            pltpu.SemaphoreType.DMA((SEL,)),
            pltpu.SemaphoreType.DMA((SEL,)),
        ],
        compiler_params=SMALL,
        name="pack_send",
    )(block_ids, layer_ids, in_hbm(grads), in_hbm(memory))


def pack_keep(block_ids, layer_ids, g_tiles, m_tiles, master, first, second):
    return pl.pallas_call(
        keep_kernel,
        out_shape=(
            jax.ShapeDtypeStruct((1024, 128), f32),
            jax.ShapeDtypeStruct((24, 128), f32),
            jax.ShapeDtypeStruct((SEL, 128), f32),
            jax.ShapeDtypeStruct((8, 128), jnp.int32),
        ),
        in_specs=[SMEM, SMEM, VMEM, VMEM, VMEM, VMEM, VMEM],
        out_specs=(VMEM, VMEM, VMEM, VMEM),
        scratch_shapes=[pltpu.VMEM((8, TILE, TILE), f32)],
        compiler_params=SMALL,
        name="pack_keep",
    )(block_ids, layer_ids, g_tiles, m_tiles, master, first, second)


PARTS = 8
ROWS = 2 * 1024 // PARTS
CHUNK = 16


def filter_kernel(
    block_ref, layer_ref, grads, memory, after, out, done, g_buf, m_buf, o_buf, g_sem, m_sem, o_sem
):
    def rows(part):
        return pl.ds(pl.multiple_of(part * ROWS, ROWS), ROWS)

    def read(part, src, buf, sem):
        return pltpu.make_async_copy(src.at[rows(part)], buf.at[rows(part)], sem.at[part])

    def write(part):
        return pltpu.make_async_copy(o_buf.at[rows(part)], out.at[rows(part)], o_sem.at[part])

    @pl.loop(0, PARTS)
    def _(part):
        read(part, grads, g_buf, g_sem).start()
        read(part, memory, m_buf, m_sem).start()

    done[...] = jnp.zeros((8, 128), f32)
    tile = iota((8, 1024), 1) // TILE

    @pl.loop(0, PARTS)
    def _(part):
        read(part, grads, g_buf, g_sem).wait()
        read(part, memory, m_buf, m_sem).wait()
        for i in range(ROWS // TILE):
            column = tile + (part * (ROWS // TILE) + i) * TILES_SIDE
            chosen = jnp.zeros((8, 1024), jnp.bool_)
            for k in range(SEL):
                chosen = jnp.logical_or(chosen, column == layer_ref[k] * BLOCKS_LAYER + block_ref[k])
            rate = jnp.where(chosen, f32(0.0), f32(filter_rate))
            rate = jnp.concatenate([rate] * (CHUNK // 8), axis=0)

            @pl.loop(0, TILE // CHUNK, unroll=TILE // CHUNK)
            def _(c):
                at = pl.ds(pl.multiple_of(part * ROWS + i * TILE + c * CHUNK, CHUNK), CHUNK)
                mem = m_buf[at, :].astype(f32)
                total = g_buf[at, :].astype(f32) + mem
                mixed = f32(1.0 - filter_rate) * mem + rate * total
                o_buf[at, :] = mixed.astype(jnp.bfloat16)

        write(part).start()

    @pl.loop(0, PARTS)
    def _(part):
        write(part).wait()


def filter_memory(block_ids, layer_ids, grads, memory, after):
    flat = (2 * 1024, 1024)
    buf = pltpu.VMEM(flat, jnp.bfloat16)
    sem = pltpu.SemaphoreType.DMA((PARTS,))
    out, done = pl.pallas_call(
        filter_kernel,
        out_shape=(jax.ShapeDtypeStruct(flat, jnp.bfloat16), jax.ShapeDtypeStruct((8, 128), f32)),
        in_specs=[SMEM, SMEM, HBM, HBM, HBM],
        out_specs=(HBM, VMEM),
        scratch_shapes=[buf, buf, buf, sem, sem, sem],
        compiler_params=LARGE,
        cost_estimate=pl.CostEstimate(flops=8 << 20, bytes_accessed=12 << 20, transcendentals=0),
        name="filter_memory",
    )(block_ids, layer_ids, in_hbm(grads.reshape(flat)), in_hbm(memory.reshape(flat)), after)
    return out.reshape(2, 1024, 1024), done


def partial_kernel(got, own, after, out_ref, tmp):
    for j in range(8):
        total = got[0, pl.ds(8 * j, 8), :]
        for s in range(1, YX):
            total = total + got[s, pl.ds(8 * j, 8), :]
        tmp[pl.ds(j, Z, stride=8), :] = total
    for z in range(Z):
        out_ref[z, pl.ds(0, 64), :] = tmp[...]
        out_ref[z, pl.ds(64, 24), :] = own[...]


def partial_sums(got, own, after):
    return pl.pallas_call(
        partial_kernel,
        out_shape=jax.ShapeDtypeStruct((Z, 88, 128), f32),
        in_specs=[VMEM, VMEM, VMEM],
        out_specs=VMEM,
        scratch_shapes=[pltpu.VMEM((64, 128), f32)],
        compiler_params=SMALL,
        name="sum_partials",
    )(got, own, after)


def update_kernel(got, out_ref, own_sum, own_update):
    me = lax.axis_index("z")
    squares = jnp.zeros((8, 128), f32)
    for z in range(Z):
        at = pl.ds(8 * z, 8)
        summed = got[0, at, :]
        for s in range(1, Z):
            summed = summed + got[s, at, :]
        first = got[z, pl.ds(64, 8), :]
        second = got[z, pl.ds(72, 8), :]
        weights = got[z, pl.ds(80, 8), :]
        first_sel = beta_one * first + (1.0 - beta_one) * summed
        second_sel = beta_two * second + (1.0 - beta_two) * summed * summed
        update = first_sel / (jnp.sqrt(second_sel) + adam_eps) + weight_decay * weights
        squares = squares + weights * weights
        for s in range(YX):
            out_ref[s, at, :] = update

        @pl.when(me == z)
        def _():
            own_sum[...] = summed
            own_update[...] = update

    for s in range(YX):
        out_ref[s, pl.ds(64, 8), :] = squares


def updates(got):
    tile = jax.ShapeDtypeStruct((8, 128), f32)
    return pl.pallas_call(
        update_kernel,
        out_shape=(jax.ShapeDtypeStruct((YX, 72, 128), f32), tile, tile),
        in_specs=[VMEM],
        out_specs=(VMEM, VMEM, VMEM),
        compiler_params=SMALL,
        name="lamb_update",
    )(got)


def state_kernel(hot_ref, own_sum, first, second, first_new, second_new):
    hot = hot_ref[...]
    named = jnp.max(hot, axis=0, keepdims=True) > 0.5
    summed = spread_entries(hot, own_sum[...])
    old = first[...]
    first_new[...] = jnp.where(named, beta_one * old + (1.0 - beta_one) * summed, old)
    old = second[...]
    second_new[...] = jnp.where(named, beta_two * old + (1.0 - beta_two) * summed * summed, old)


def new_moments(hot, own_sum, first, second):
    state = jax.ShapeDtypeStruct((HALF, 128), f32)
    return pl.pallas_call(
        state_kernel,
        out_shape=(state, state),
        in_specs=[VMEM] * 4,
        out_specs=(VMEM, VMEM),
        compiler_params=SMALL,
        name="new_moments",
    )(hot, own_sum, first, second)


CHUNKS = 4
WIDTH = TILE * TILE // CHUNKS


def step_kernel(layers_ref, hot_ref, own, other, own_update, master, step_ref, master_new, buf, sem):
    update_sq = [jnp.zeros((8, 128), f32) for _ in range(4)]
    weight_sq = jnp.zeros((8, 128), f32)
    for ref in (own, other):
        for s in range(YX):
            for z in range(Z):
                value = ref[s, pl.ds(8 * z, 8), :]
                update_sq[z % 4] = update_sq[z % 4] + value * value
            weight_sq = weight_sq + ref[s, pl.ds(64, 8), :]
    update_sq = (update_sq[0] + update_sq[1]) + (update_sq[2] + update_sq[3])
    layer = layers_ref[...]
    ratio = jnp.zeros((8, 128), f32)
    for which in range(2):
        mine = layer == which
        weight_total = jnp.sum(jnp.where(mine, weight_sq, 0.0), keepdims=True)
        update_total = jnp.sum(jnp.where(mine, update_sq, 0.0), keepdims=True)
        ratio = jnp.where(mine, jnp.sqrt(weight_total / (update_total + norm_eps)), ratio)
    low = iota((8, 128), 1) < HALF
    first_core = lax.axis_index("c") == 0

    def chunk(i):
        at = pl.ds(i * WIDTH, WIDTH)
        return pltpu.make_async_copy(buf.at[:, at], step_ref.at[:, at], sem.at[i])

    for y in range(Y):
        for z in range(Z):
            for x in range(X):
                at = (y * X + x, pl.ds(8 * z, 8))
                a = ratio * own[at]
                b = ratio * other[at]
                turned = pltpu.roll(jnp.where(first_core, b, a), HALF, 1)
                straight = jnp.where(first_core, a, b)
                top = jnp.where(low, straight, turned)
                bottom = jnp.where(low, pltpu.roll(straight, HALF, 1), jnp.where(first_core, b, a))
                row = (y * Z + z) * X + x
                buf[:, pl.ds(row * TILE, TILE)] = jnp.concatenate([top, bottom], axis=0).astype(jnp.bfloat16)
        chunk(y).start()
    hot = hot_ref[...]
    named = jnp.max(hot, axis=0, keepdims=True) > 0.5
    scaled = spread_entries(hot, ratio * own_update[...])
    old = master[...]
    master_new[...] = jnp.where(named, old - learn_rate * scaled, old)
    for i in range(CHUNKS):
        chunk(i).wait()


def steps(layers, hot, own, other, own_update, master):
    step = (SEL, TILE * TILE)
    return pl.pallas_call(
        step_kernel,
        out_shape=(jax.ShapeDtypeStruct(step, jnp.bfloat16), jax.ShapeDtypeStruct((HALF, 128), f32)),
        in_specs=[VMEM] * 6,
        out_specs=(HBM, VMEM),
        scratch_shapes=[pltpu.VMEM(step, jnp.bfloat16), pltpu.SemaphoreType.DMA((CHUNKS,))],
        compiler_params=SMALL,
        name="scaled_step",
    )(layers, hot, own, other, own_update, master)


def on_device(grads, memory, block_ids, layer_ids, master, first_moment, second_moment):
    swap = [(0, 1), (1, 0)]
    block_ids, layer_ids = in_hbm(block_ids), in_hbm(layer_ids)
    master, first, second = master.T, first_moment.T, second_moment.T
    send, g_tiles, m_tiles = pack_send(block_ids, layer_ids, grads, memory)
    received = lax.ppermute(send, "c", swap)
    keep, own, hot, layers = pack_keep(block_ids, layer_ids, g_tiles, m_tiles, master, first, second)
    part = (keep + received).reshape(YX, 64, 128)
    new_memory, done = filter_memory(block_ids, layer_ids, grads, memory, part)
    got = lax.all_to_all(part, ("y", "x"), 0, 0, tiled=True)
    sums = partial_sums(got, own, done)
    got = lax.all_to_all(sums, "z", 0, 0, tiled=True)
    payload, own_sum, own_update = updates(got)
    mine = lax.all_to_all(payload, ("y", "x"), 0, 0, tiled=True)
    other = lax.ppermute(mine, "c", swap)
    first_new, second_new = new_moments(hot, own_sum, first, second)
    step_blocks, master_new = steps(layers, hot, mine, other, own_update, master)
    return (new_memory, master_new.T, first_new.T, second_new.T, step_blocks)


def solution(mesh):
    torus = Mesh(mesh.devices.reshape(Y, Z, X, C), ("y", "z", "x", "c"))
    dp = ("y", "z", "x", "c")
    replica = P(dp, None, None)
    state = P(None, dp)
    return jax.shard_map(
        on_device,
        mesh=torus,
        in_specs=(replica, replica, P(), P(), state, state, state),
        out_specs=(replica, state, state, state, P()),
        check_vma=False,
    )
```

```python
import functools

import jax
import jax.numpy as jnp
from jax import lax
from jax.experimental import pallas as pl
from jax.experimental.pallas import tpu as pltpu
from jax.sharding import PartitionSpec as P

TILE = 128
SEL = 16
HALF = 64
Y, Z, X, C = 4, 8, 4, 2
YX = Y * X
TILES_SIDE = 8
BLOCKS_LAYER = 64

filter_rate = 0.3
beta_one = 0.9
beta_two = 0.999
adam_eps = 1e-06
weight_decay = 0.01
learn_rate = 0.01
norm_eps = 1e-06


def device(y, z, x, c):
    return ((y * Z + z) * X + x) * C + c


Z_ORDER = tuple(reversed(range(Z)))
YX_ORDER = tuple((y, x) for y in reversed(range(Y)) for x in reversed(range(X)))
Z_GROUPS = [[device(y, z, x, c) for z in Z_ORDER] for y in range(Y) for x in range(X) for c in range(C)]
YX_GROUPS = [[device(y, z, x, c) for y, x in YX_ORDER] for z in range(Z) for c in range(C)]
SWAP = [(i, i ^ 1) for i in range(Y * Z * X * C)]

f32 = jnp.float32
VMEM = pl.BlockSpec(memory_space=pltpu.VMEM)
SMEM = pl.BlockSpec(memory_space=pltpu.SMEM)
HBM = pl.BlockSpec(memory_space=pl.ANY)
LARGE = pltpu.CompilerParams(vmem_limit_bytes=16 << 20)
SMALL = pltpu.CompilerParams(vmem_limit_bytes=8 << 20)


def in_hbm(array):
    return pltpu.with_memory_space_constraint(array, pltpu.HBM)


def iota(shape, dim):
    return lax.broadcasted_iota(jnp.int32, shape, dim)


def one_hot(block_ref, layer_ref):
    sub = iota((SEL, 128), 0)
    column = jnp.zeros((SEL, 128), jnp.int32)
    for k in range(SEL):
        column = jnp.where(sub == k, layer_ref[k] * BLOCKS_LAYER + block_ref[k], column)
    return (column == iota((SEL, 128), 1)).astype(f32)


def layer_tile(layer_ref):
    sub = iota((8, 128), 0)
    low = iota((8, 128), 1) < HALF
    layer = jnp.zeros((8, 128), jnp.int32)
    for k in range(8):
        layer = jnp.where(sub == k, jnp.where(low, layer_ref[k], layer_ref[k + 8]), layer)
    return layer


def select_entries(hot, state):
    picked = lax.dot_general(
        hot, state, (((1,), (1,)), ((), ())), precision=lax.Precision.HIGHEST, preferred_element_type=f32
    )
    return jnp.concatenate([picked[:8], picked[8:]], axis=1)


def spread_entries(hot, tile):
    rows = jnp.concatenate([tile[:, :HALF], tile[:, HALF:]], axis=0)
    return lax.dot_general(
        rows, hot, (((0,), (0,)), ((), ())), precision=lax.Precision.HIGHEST, preferred_element_type=f32
    )


def half_columns(g_tiles, m_tiles, j, left):
    low = iota((TILE, TILE), 1) < HALF
    a = g_tiles[j].astype(f32) + m_tiles[j].astype(f32)
    b = g_tiles[j + 8].astype(f32) + m_tiles[j + 8].astype(f32)
    turned = pltpu.roll(jnp.where(left, b, a), HALF, 1)
    return jnp.where(low, jnp.where(left, a, turned), jnp.where(left, turned, b))


def store_rows(out_ref, tmp, j, value):
    tmp[j] = value
    for y in range(Y):
        for x in range(X):
            out_ref[pl.ds(YX_ORDER.index((y, x)) * 64 + j * 8, 8), :] = tmp[j, pl.ds(y * Z * X + x, Z, stride=X), :]


def send_kernel(block_ref, layer_ref, grads, memory, send_ref, g_tiles, m_tiles, tmp, g_sem, m_sem):
    copies = []
    for k in (j + 8 * h for j in range(8) for h in range(2)):
        layer = layer_ref[k]
        row = pl.multiple_of((block_ref[k] // TILES_SIDE) * TILE, TILE)
        col = pl.multiple_of((block_ref[k] % TILES_SIDE) * TILE, TILE)
        at = (layer, pl.ds(row, TILE), pl.ds(col, TILE))
        for src, buf, sem in ((grads, g_tiles, g_sem), (memory, m_tiles, m_sem)):
            copy = pltpu.make_async_copy(src.at[at], buf.at[k], sem.at[k])
            copy.start()
            copies.append(copy)
    for j in range(8):
        for copy in copies[4 * j : 4 * j + 4]:
            copy.wait()
        store_rows(send_ref, tmp, j, half_columns(g_tiles, m_tiles, j, lax.axis_index("dp") % C == 1))


def keep_kernel(block_ref, layer_ref, g_tiles, m_tiles, master, first, second, keep_ref, own_ref, hot_ref, layers_ref, tmp):
    for j in range(8):
        store_rows(keep_ref, tmp, j, half_columns(g_tiles, m_tiles, j, lax.axis_index("dp") % C == 0))
    hot = one_hot(block_ref, layer_ref)
    hot_ref[...] = hot
    layers_ref[...] = layer_tile(layer_ref)
    for i, state in enumerate((first, second, master)):
        own_ref[pl.ds(8 * i, 8), :] = select_entries(hot, state[...])


def pack_send(block_ids, layer_ids, grads, memory):
    tiles = jax.ShapeDtypeStruct((SEL, TILE, TILE), jnp.bfloat16)
    return pl.pallas_call(
        send_kernel,
        out_shape=(jax.ShapeDtypeStruct((1024, 128), f32), tiles, tiles),
        in_specs=[SMEM, SMEM, HBM, HBM],
        out_specs=(VMEM, VMEM, VMEM),
        scratch_shapes=[
            pltpu.VMEM((8, TILE, TILE), f32),
            pltpu.SemaphoreType.DMA((SEL,)),
            pltpu.SemaphoreType.DMA((SEL,)),
        ],
        compiler_params=SMALL,
        name="pack_send",
    )(block_ids, layer_ids, in_hbm(grads), in_hbm(memory))


def pack_keep(block_ids, layer_ids, g_tiles, m_tiles, master, first, second):
    return pl.pallas_call(
        keep_kernel,
        out_shape=(
            jax.ShapeDtypeStruct((1024, 128), f32),
            jax.ShapeDtypeStruct((24, 128), f32),
            jax.ShapeDtypeStruct((SEL, 128), f32),
            jax.ShapeDtypeStruct((8, 128), jnp.int32),
        ),
        in_specs=[SMEM, SMEM, VMEM, VMEM, VMEM, VMEM, VMEM],
        out_specs=(VMEM, VMEM, VMEM, VMEM),
        scratch_shapes=[pltpu.VMEM((8, TILE, TILE), f32)],
        compiler_params=SMALL,
        name="pack_keep",
    )(block_ids, layer_ids, g_tiles, m_tiles, master, first, second)


PARTS = 8
ROWS = 2 * 1024 // PARTS
CHUNK = 16


def filter_kernel(
    block_ref, layer_ref, grads, memory, after, out, done, g_buf, m_buf, o_buf, g_sem, m_sem, o_sem
):
    def rows(part):
        return pl.ds(pl.multiple_of(part * ROWS, ROWS), ROWS)

    def read(part, src, buf, sem):
        return pltpu.make_async_copy(src.at[rows(part)], buf.at[rows(part)], sem.at[part])

    def write(part):
        return pltpu.make_async_copy(o_buf.at[rows(part)], out.at[rows(part)], o_sem.at[part])

    @pl.loop(0, PARTS)
    def _(part):
        read(part, grads, g_buf, g_sem).start()
        read(part, memory, m_buf, m_sem).start()

    done[...] = jnp.zeros((8, 128), f32)
    tile = iota((8, 1024), 1) // TILE

    @pl.loop(0, PARTS)
    def _(part):
        read(part, grads, g_buf, g_sem).wait()
        read(part, memory, m_buf, m_sem).wait()
        for i in range(ROWS // TILE):
            column = tile + (part * (ROWS // TILE) + i) * TILES_SIDE
            chosen = jnp.zeros((8, 1024), jnp.bool_)
            for k in range(SEL):
                chosen = jnp.logical_or(chosen, column == layer_ref[k] * BLOCKS_LAYER + block_ref[k])
            rate = jnp.where(chosen, f32(0.0), f32(filter_rate))
            rate = jnp.concatenate([rate] * (CHUNK // 8), axis=0)

            @pl.loop(0, TILE // CHUNK, unroll=TILE // CHUNK)
            def _(c):
                at = pl.ds(pl.multiple_of(part * ROWS + i * TILE + c * CHUNK, CHUNK), CHUNK)
                mem = m_buf[at, :].astype(f32)
                total = g_buf[at, :].astype(f32) + mem
                mixed = f32(1.0 - filter_rate) * mem + rate * total
                o_buf[at, :] = mixed.astype(jnp.bfloat16)

        write(part).start()

    @pl.loop(0, PARTS)
    def _(part):
        write(part).wait()


def filter_memory(block_ids, layer_ids, grads, memory, after):
    flat = (2 * 1024, 1024)
    buf = pltpu.VMEM(flat, jnp.bfloat16)
    sem = pltpu.SemaphoreType.DMA((PARTS,))
    out, done = pl.pallas_call(
        filter_kernel,
        out_shape=(jax.ShapeDtypeStruct(flat, jnp.bfloat16), jax.ShapeDtypeStruct((8, 128), f32)),
        in_specs=[SMEM, SMEM, HBM, HBM, HBM],
        out_specs=(HBM, VMEM),
        scratch_shapes=[buf, buf, buf, sem, sem, sem],
        compiler_params=LARGE,
        cost_estimate=pl.CostEstimate(flops=8 << 20, bytes_accessed=12 << 20, transcendentals=0),
        name="filter_memory",
    )(block_ids, layer_ids, in_hbm(grads.reshape(flat)), in_hbm(memory.reshape(flat)), after)
    return out.reshape(2, 1024, 1024), done


def partial_kernel(got, own, after, out_ref, tmp):
    for j in range(8):
        total = got[0, pl.ds(8 * j, 8), :]
        for s in range(1, YX):
            total = total + got[s, pl.ds(8 * j, 8), :]
        tmp[pl.ds(j, Z, stride=8), :] = total
    for z in range(Z):
        out_ref[z, pl.ds(0, 64), :] = tmp[...]
        out_ref[z, pl.ds(64, 24), :] = own[...]


def partial_sums(got, own, after):
    return pl.pallas_call(
        partial_kernel,
        out_shape=jax.ShapeDtypeStruct((Z, 88, 128), f32),
        in_specs=[VMEM, VMEM, VMEM],
        out_specs=VMEM,
        scratch_shapes=[pltpu.VMEM((64, 128), f32)],
        compiler_params=SMALL,
        name="sum_partials",
    )(got, own, after)


def update_kernel(got, out_ref, own_sum, own_update):
    me = lax.axis_index("dp") // (X * C) % Z
    squares = jnp.zeros((8, 128), f32)
    for z in range(Z):
        at = pl.ds(8 * z, 8)
        summed = got[0, at, :]
        for s in range(1, Z):
            summed = summed + got[s, at, :]
        first = got[Z_ORDER.index(z), pl.ds(64, 8), :]
        second = got[Z_ORDER.index(z), pl.ds(72, 8), :]
        weights = got[Z_ORDER.index(z), pl.ds(80, 8), :]
        first_sel = beta_one * first + (1.0 - beta_one) * summed
        second_sel = beta_two * second + (1.0 - beta_two) * summed * summed
        update = first_sel / (jnp.sqrt(second_sel) + adam_eps) + weight_decay * weights
        squares = squares + weights * weights
        for s in range(YX):
            out_ref[s, at, :] = update

        @pl.when(me == z)
        def _():
            own_sum[...] = summed
            own_update[...] = update

    for s in range(YX):
        out_ref[s, pl.ds(64, 8), :] = squares


def updates(got):
    tile = jax.ShapeDtypeStruct((8, 128), f32)
    return pl.pallas_call(
        update_kernel,
        out_shape=(jax.ShapeDtypeStruct((YX, 72, 128), f32), tile, tile),
        in_specs=[VMEM],
        out_specs=(VMEM, VMEM, VMEM),
        compiler_params=SMALL,
        name="lamb_update",
    )(got)


def state_kernel(hot_ref, own_sum, first, second, first_new, second_new):
    hot = hot_ref[...]
    named = jnp.max(hot, axis=0, keepdims=True) > 0.5
    summed = spread_entries(hot, own_sum[...])
    old = first[...]
    first_new[...] = jnp.where(named, beta_one * old + (1.0 - beta_one) * summed, old)
    old = second[...]
    second_new[...] = jnp.where(named, beta_two * old + (1.0 - beta_two) * summed * summed, old)


def new_moments(hot, own_sum, first, second):
    state = jax.ShapeDtypeStruct((HALF, 128), f32)
    return pl.pallas_call(
        state_kernel,
        out_shape=(state, state),
        in_specs=[VMEM] * 4,
        out_specs=(VMEM, VMEM),
        compiler_params=SMALL,
        name="new_moments",
    )(hot, own_sum, first, second)


CHUNKS = 4
WIDTH = TILE * TILE // CHUNKS


def step_kernel(layers_ref, hot_ref, own, other, own_update, master, step_ref, master_new, buf, sem):
    update_sq = [jnp.zeros((8, 128), f32) for _ in range(4)]
    weight_sq = jnp.zeros((8, 128), f32)
    for ref in (own, other):
        for s in range(YX):
            for z in range(Z):
                value = ref[s, pl.ds(8 * z, 8), :]
                update_sq[z % 4] = update_sq[z % 4] + value * value
            weight_sq = weight_sq + ref[s, pl.ds(64, 8), :]
    update_sq = (update_sq[0] + update_sq[1]) + (update_sq[2] + update_sq[3])
    layer = layers_ref[...]
    ratio = jnp.zeros((8, 128), f32)
    for which in range(2):
        mine = layer == which
        weight_total = jnp.sum(jnp.where(mine, weight_sq, 0.0), keepdims=True)
        update_total = jnp.sum(jnp.where(mine, update_sq, 0.0), keepdims=True)
        ratio = jnp.where(mine, jnp.sqrt(weight_total / (update_total + norm_eps)), ratio)
    low = iota((8, 128), 1) < HALF
    first_core = lax.axis_index("dp") % C == 0

    def chunk(i):
        at = pl.ds(i * WIDTH, WIDTH)
        return pltpu.make_async_copy(buf.at[:, at], step_ref.at[:, at], sem.at[i])

    for y in range(Y):
        for z in range(Z):
            for x in range(X):
                at = (YX_ORDER.index((y, x)), pl.ds(8 * z, 8))
                a = ratio * own[at]
                b = ratio * other[at]
                turned = pltpu.roll(jnp.where(first_core, b, a), HALF, 1)
                straight = jnp.where(first_core, a, b)
                top = jnp.where(low, straight, turned)
                bottom = jnp.where(low, pltpu.roll(straight, HALF, 1), jnp.where(first_core, b, a))
                row = (y * Z + z) * X + x
                buf[:, pl.ds(row * TILE, TILE)] = jnp.concatenate([top, bottom], axis=0).astype(jnp.bfloat16)
        chunk(y).start()
    hot = hot_ref[...]
    named = jnp.max(hot, axis=0, keepdims=True) > 0.5
    scaled = spread_entries(hot, ratio * own_update[...])
    old = master[...]
    master_new[...] = jnp.where(named, old - learn_rate * scaled, old)
    for i in range(CHUNKS):
        chunk(i).wait()


def steps(layers, hot, own, other, own_update, master):
    step = (SEL, TILE * TILE)
    return pl.pallas_call(
        step_kernel,
        out_shape=(jax.ShapeDtypeStruct(step, jnp.bfloat16), jax.ShapeDtypeStruct((HALF, 128), f32)),
        in_specs=[VMEM] * 6,
        out_specs=(HBM, VMEM),
        scratch_shapes=[pltpu.VMEM(step, jnp.bfloat16), pltpu.SemaphoreType.DMA((CHUNKS,))],
        compiler_params=SMALL,
        name="scaled_step",
    )(layers, hot, own, other, own_update, master)


def on_device(grads, memory, block_ids, layer_ids, master, first_moment, second_moment):
    block_ids, layer_ids = in_hbm(block_ids), in_hbm(layer_ids)
    master, first, second = master.T, first_moment.T, second_moment.T
    send, g_tiles, m_tiles = pack_send(block_ids, layer_ids, grads, memory)
    received = lax.ppermute(send, "dp", SWAP)
    keep, own, hot, layers = pack_keep(block_ids, layer_ids, g_tiles, m_tiles, master, first, second)
    part = (keep + received).reshape(YX, 64, 128)
    new_memory, done = filter_memory(block_ids, layer_ids, grads, memory, part)
    got = lax.all_to_all(part, "dp", 0, 0, axis_index_groups=YX_GROUPS, tiled=True)
    sums = partial_sums(got, own, done)
    got = lax.all_to_all(sums, "dp", 0, 0, axis_index_groups=Z_GROUPS, tiled=True)
    payload, own_sum, own_update = updates(got)
    mine = lax.all_to_all(payload, "dp", 0, 0, axis_index_groups=YX_GROUPS, tiled=True)
    other = lax.ppermute(mine, "dp", SWAP)
    first_new, second_new = new_moments(hot, own_sum, first, second)
    step_blocks, master_new = steps(layers, hot, mine, other, own_update, master)
    return (new_memory, master_new.T, first_new.T, second_new.T, step_blocks)


def solution(mesh):
    replica = P("dp", None, None)
    state = P(None, "dp")
    return jax.shard_map(
        on_device,
        mesh=mesh,
        in_specs=(replica, replica, P(), P(), state, state, state),
        out_specs=(replica, state, state, state, P()),
        check_vma=False,
    )
```

```python
import functools

import jax
import jax.numpy as jnp
from jax import lax
from jax.experimental import pallas as pl
from jax.experimental.pallas import tpu as pltpu
from jax.sharding import PartitionSpec as P

TILE = 128
SEL = 16
HALF = 64
Y, Z, X, C = 4, 8, 4, 2
YX = Y * X
TILES_SIDE = 8
BLOCKS_LAYER = 64

filter_rate = 0.3
beta_one = 0.9
beta_two = 0.999
adam_eps = 1e-06
weight_decay = 0.01
learn_rate = 0.01
norm_eps = 1e-06


def device(y, z, x, c):
    return ((y * Z + z) * X + x) * C + c


Z_ORDER = tuple(reversed(range(Z)))
YX_ORDER = tuple((y, x) for y in reversed(range(Y)) for x in reversed(range(X)))
Z_GROUPS = [[device(y, z, x, c) for z in Z_ORDER] for y in range(Y) for x in range(X) for c in range(C)]
YX_GROUPS = [[device(y, z, x, c) for y, x in YX_ORDER] for z in range(Z) for c in range(C)]
SWAP = [(i, i ^ 1) for i in range(Y * Z * X * C)]

f32 = jnp.float32
VMEM = pl.BlockSpec(memory_space=pltpu.VMEM)
SMEM = pl.BlockSpec(memory_space=pltpu.SMEM)
HBM = pl.BlockSpec(memory_space=pl.ANY)
LARGE = pltpu.CompilerParams(vmem_limit_bytes=16 << 20)
SMALL = pltpu.CompilerParams(vmem_limit_bytes=8 << 20)


def in_hbm(array):
    return pltpu.with_memory_space_constraint(array, pltpu.HBM)


def iota(shape, dim):
    return lax.broadcasted_iota(jnp.int32, shape, dim)


def one_hot(block_ref, layer_ref):
    sub = iota((SEL, 128), 0)
    column = jnp.zeros((SEL, 128), jnp.int32)
    for k in range(SEL):
        column = jnp.where(sub == k, layer_ref[k] * BLOCKS_LAYER + block_ref[k], column)
    return (column == iota((SEL, 128), 1)).astype(f32)


def layer_tile(layer_ref):
    sub = iota((8, 128), 0)
    low = iota((8, 128), 1) < HALF
    layer = jnp.zeros((8, 128), jnp.int32)
    for k in range(8):
        layer = jnp.where(sub == k, jnp.where(low, layer_ref[k], layer_ref[k + 8]), layer)
    return layer


def select_entries(hot, state):
    picked = lax.dot_general(
        hot, state, (((1,), (1,)), ((), ())), precision=lax.Precision.HIGHEST, preferred_element_type=f32
    )
    return jnp.concatenate([picked[:8], picked[8:]], axis=1)


def spread_entries(hot, tile):
    rows = jnp.concatenate([tile[:, :HALF], tile[:, HALF:]], axis=0)
    return lax.dot_general(
        rows, hot, (((0,), (0,)), ((), ())), precision=lax.Precision.HIGHEST, preferred_element_type=f32
    )


def half_columns(g_tiles, m_tiles, j, left):
    low = iota((TILE, TILE), 1) < HALF
    a = g_tiles[j].astype(f32) + m_tiles[j].astype(f32)
    b = g_tiles[j + 8].astype(f32) + m_tiles[j + 8].astype(f32)
    turned = pltpu.roll(jnp.where(left, b, a), HALF, 1)
    return jnp.where(low, jnp.where(left, a, turned), jnp.where(left, turned, b))


def store_rows(out_ref, tmp, j, value):
    tmp[j, pl.ds(0, TILE), :] = value
    for y in range(Y):
        for x in range(X):
            out_ref[pl.ds(YX_ORDER.index((y, x)) * 64 + j * 8, 8), :] = tmp[j, pl.ds(y * Z * X + x, Z, stride=X), :]


def send_kernel(block_ref, layer_ref, grads, memory, send_ref, g_tiles, m_tiles, tmp, g_sem, m_sem):
    copies = []
    for k in (j + 8 * h for j in range(8) for h in range(2)):
        layer = layer_ref[k]
        row = pl.multiple_of((block_ref[k] // TILES_SIDE) * TILE, TILE)
        col = pl.multiple_of((block_ref[k] % TILES_SIDE) * TILE, TILE)
        at = (layer, pl.ds(row, TILE), pl.ds(col, TILE))
        for src, buf, sem in ((grads, g_tiles, g_sem), (memory, m_tiles, m_sem)):
            copy = pltpu.make_async_copy(src.at[at], buf.at[k], sem.at[k])
            copy.start()
            copies.append(copy)
    for j in range(8):
        for copy in copies[4 * j : 4 * j + 4]:
            copy.wait()
        store_rows(send_ref, tmp, j, half_columns(g_tiles, m_tiles, j, lax.axis_index("dp") % C == 1))


def keep_kernel(block_ref, layer_ref, g_tiles, m_tiles, master, first, second, keep_ref, own_ref, hot_ref, layers_ref, tmp):
    for j in range(8):
        store_rows(keep_ref, tmp, j, half_columns(g_tiles, m_tiles, j, lax.axis_index("dp") % C == 0))
    hot = one_hot(block_ref, layer_ref)
    hot_ref[...] = hot
    layers_ref[...] = layer_tile(layer_ref)
    for i, state in enumerate((first, second, master)):
        own_ref[pl.ds(8 * i, 8), :] = select_entries(hot, state[...])


def pack_send(block_ids, layer_ids, grads, memory):
    tiles = jax.ShapeDtypeStruct((SEL, TILE, TILE), jnp.bfloat16)
    return pl.pallas_call(
        send_kernel,
        out_shape=(jax.ShapeDtypeStruct((1024, 128), f32), tiles, tiles),
        in_specs=[SMEM, SMEM, HBM, HBM],
        out_specs=(VMEM, VMEM, VMEM),
        scratch_shapes=[
            pltpu.VMEM((8, TILE + 8, TILE), f32),
            pltpu.SemaphoreType.DMA((SEL,)),
            pltpu.SemaphoreType.DMA((SEL,)),
        ],
        compiler_params=SMALL,
        name="pack_send",
    )(block_ids, layer_ids, in_hbm(grads), in_hbm(memory))


def pack_keep(block_ids, layer_ids, g_tiles, m_tiles, master, first, second):
    return pl.pallas_call(
        keep_kernel,
        out_shape=(
            jax.ShapeDtypeStruct((1024, 128), f32),
            jax.ShapeDtypeStruct((24, 128), f32),
            jax.ShapeDtypeStruct((SEL, 128), f32),
            jax.ShapeDtypeStruct((8, 128), jnp.int32),
        ),
        in_specs=[SMEM, SMEM, VMEM, VMEM, VMEM, VMEM, VMEM],
        out_specs=(VMEM, VMEM, VMEM, VMEM),
        scratch_shapes=[pltpu.VMEM((8, TILE + 8, TILE), f32)],
        compiler_params=SMALL,
        name="pack_keep",
    )(block_ids, layer_ids, g_tiles, m_tiles, master, first, second)


PARTS = 8
ROWS = 2 * 1024 // PARTS
CHUNK = 16


def filter_kernel(
    block_ref, layer_ref, grads, memory, after, out, done, g_buf, m_buf, o_buf, g_sem, m_sem, o_sem
):
    def rows(part):
        return pl.ds(pl.multiple_of(part * ROWS, ROWS), ROWS)

    def read(part, src, buf, sem):
        return pltpu.make_async_copy(src.at[rows(part)], buf.at[rows(part)], sem.at[part])

    def write(part):
        return pltpu.make_async_copy(o_buf.at[rows(part)], out.at[rows(part)], o_sem.at[part])

    @pl.loop(0, PARTS)
    def _(part):
        read(part, grads, g_buf, g_sem).start()
        read(part, memory, m_buf, m_sem).start()

    done[...] = jnp.zeros((8, 128), f32)
    tile = iota((8, 1024), 1) // TILE

    @pl.loop(0, PARTS)
    def _(part):
        read(part, grads, g_buf, g_sem).wait()
        read(part, memory, m_buf, m_sem).wait()
        for i in range(ROWS // TILE):
            column = tile + (part * (ROWS // TILE) + i) * TILES_SIDE
            chosen = jnp.zeros((8, 1024), jnp.bool_)
            for k in range(SEL):
                chosen = jnp.logical_or(chosen, column == layer_ref[k] * BLOCKS_LAYER + block_ref[k])
            rate = jnp.where(chosen, f32(0.0), f32(filter_rate))
            rate = jnp.concatenate([rate] * (CHUNK // 8), axis=0)

            @pl.loop(0, TILE // CHUNK, unroll=TILE // CHUNK)
            def _(c):
                at = pl.ds(pl.multiple_of(part * ROWS + i * TILE + c * CHUNK, CHUNK), CHUNK)
                mem = m_buf[at, :].astype(f32)
                total = g_buf[at, :].astype(f32) + mem
                mixed = f32(1.0 - filter_rate) * mem + rate * total
                o_buf[at, :] = mixed.astype(jnp.bfloat16)

        write(part).start()

    @pl.loop(0, PARTS)
    def _(part):
        write(part).wait()


def filter_memory(block_ids, layer_ids, grads, memory, after):
    flat = (2 * 1024, 1024)
    buf = pltpu.VMEM(flat, jnp.bfloat16)
    sem = pltpu.SemaphoreType.DMA((PARTS,))
    out, done = pl.pallas_call(
        filter_kernel,
        out_shape=(jax.ShapeDtypeStruct(flat, jnp.bfloat16), jax.ShapeDtypeStruct((8, 128), f32)),
        in_specs=[SMEM, SMEM, HBM, HBM, HBM],
        out_specs=(HBM, VMEM),
        scratch_shapes=[buf, buf, buf, sem, sem, sem],
        compiler_params=LARGE,
        cost_estimate=pl.CostEstimate(flops=8 << 20, bytes_accessed=12 << 20, transcendentals=0),
        name="filter_memory",
    )(block_ids, layer_ids, in_hbm(grads.reshape(flat)), in_hbm(memory.reshape(flat)), after)
    return out.reshape(2, 1024, 1024), done


def partial_kernel(got, own, after, out_ref, tmp):
    for j in range(8):
        total = got[0, pl.ds(8 * j, 8), :]
        for s in range(1, YX):
            total = total + got[s, pl.ds(8 * j, 8), :]
        tmp[pl.ds(j, Z, stride=8), :] = total
    for z in range(Z):
        out_ref[z, pl.ds(0, 64), :] = tmp[pl.ds(0, 64), :]
        out_ref[z, pl.ds(64, 24), :] = own[...]


def partial_sums(got, own, after):
    return pl.pallas_call(
        partial_kernel,
        out_shape=jax.ShapeDtypeStruct((Z, 88, 128), f32),
        in_specs=[VMEM, VMEM, VMEM],
        out_specs=VMEM,
        scratch_shapes=[pltpu.VMEM((72, 128), f32)],
        compiler_params=SMALL,
        name="sum_partials",
    )(got, own, after)


def update_kernel(got, out_ref, own_sum, own_update):
    me = lax.axis_index("dp") // (X * C) % Z
    squares = jnp.zeros((8, 128), f32)
    for z in range(Z):
        at = pl.ds(8 * z, 8)
        summed = got[0, at, :]
        for s in range(1, Z):
            summed = summed + got[s, at, :]
        first = got[Z_ORDER.index(z), pl.ds(64, 8), :]
        second = got[Z_ORDER.index(z), pl.ds(72, 8), :]
        weights = got[Z_ORDER.index(z), pl.ds(80, 8), :]
        first_sel = beta_one * first + (1.0 - beta_one) * summed
        second_sel = beta_two * second + (1.0 - beta_two) * summed * summed
        update = first_sel / (jnp.sqrt(second_sel) + adam_eps) + weight_decay * weights
        squares = squares + weights * weights
        for s in range(YX):
            out_ref[s, at, :] = update

        @pl.when(me == z)
        def _():
            own_sum[...] = summed
            own_update[...] = update

    for s in range(YX):
        out_ref[s, pl.ds(64, 8), :] = squares


def updates(got):
    tile = jax.ShapeDtypeStruct((8, 128), f32)
    return pl.pallas_call(
        update_kernel,
        out_shape=(jax.ShapeDtypeStruct((YX, 72, 128), f32), tile, tile),
        in_specs=[VMEM],
        out_specs=(VMEM, VMEM, VMEM),
        compiler_params=SMALL,
        name="lamb_update",
    )(got)


def state_kernel(hot_ref, own_sum, first, second, first_new, second_new):
    hot = hot_ref[...]
    named = jnp.max(hot, axis=0, keepdims=True) > 0.5
    summed = spread_entries(hot, own_sum[...])
    old = first[...]
    first_new[...] = jnp.where(named, beta_one * old + (1.0 - beta_one) * summed, old)
    old = second[...]
    second_new[...] = jnp.where(named, beta_two * old + (1.0 - beta_two) * summed * summed, old)


def new_moments(hot, own_sum, first, second):
    state = jax.ShapeDtypeStruct((HALF, 128), f32)
    return pl.pallas_call(
        state_kernel,
        out_shape=(state, state),
        in_specs=[VMEM] * 4,
        out_specs=(VMEM, VMEM),
        compiler_params=SMALL,
        name="new_moments",
    )(hot, own_sum, first, second)


CHUNKS = 4
WIDTH = TILE * TILE // CHUNKS


def step_kernel(layers_ref, hot_ref, own, other, own_update, master, step_ref, master_new, buf, sem):
    update_sq = [jnp.zeros((8, 128), f32) for _ in range(4)]
    weight_sq = jnp.zeros((8, 128), f32)
    for ref in (own, other):
        for s in range(YX):
            for z in range(Z):
                value = ref[s, pl.ds(8 * z, 8), :]
                update_sq[z % 4] = update_sq[z % 4] + value * value
            weight_sq = weight_sq + ref[s, pl.ds(64, 8), :]
    update_sq = (update_sq[0] + update_sq[1]) + (update_sq[2] + update_sq[3])
    layer = layers_ref[...]
    ratio = jnp.zeros((8, 128), f32)
    for which in range(2):
        mine = layer == which
        weight_total = jnp.sum(jnp.where(mine, weight_sq, 0.0), keepdims=True)
        update_total = jnp.sum(jnp.where(mine, update_sq, 0.0), keepdims=True)
        ratio = jnp.where(mine, jnp.sqrt(weight_total / (update_total + norm_eps)), ratio)
    low = iota((8, 128), 1) < HALF
    first_core = lax.axis_index("dp") % C == 0

    def chunk(i):
        at = pl.ds(i * WIDTH, WIDTH)
        return pltpu.make_async_copy(buf.at[:, at], step_ref.at[:, at], sem.at[i])

    for y in range(Y):
        for z in range(Z):
            for x in range(X):
                at = (YX_ORDER.index((y, x)), pl.ds(8 * z, 8))
                a = ratio * own[at]
                b = ratio * other[at]
                turned = pltpu.roll(jnp.where(first_core, b, a), HALF, 1)
                straight = jnp.where(first_core, a, b)
                top = jnp.where(low, straight, turned)
                bottom = jnp.where(low, pltpu.roll(straight, HALF, 1), jnp.where(first_core, b, a))
                row = (y * Z + z) * X + x
                buf[:, pl.ds(row * TILE, TILE)] = jnp.concatenate([top, bottom], axis=0).astype(jnp.bfloat16)
        chunk(y).start()
    hot = hot_ref[...]
    named = jnp.max(hot, axis=0, keepdims=True) > 0.5
    scaled = spread_entries(hot, ratio * own_update[...])
    old = master[...]
    master_new[...] = jnp.where(named, old - learn_rate * scaled, old)
    for i in range(CHUNKS):
        chunk(i).wait()


def steps(layers, hot, own, other, own_update, master):
    step = (SEL, TILE * TILE)
    return pl.pallas_call(
        step_kernel,
        out_shape=(jax.ShapeDtypeStruct(step, jnp.bfloat16), jax.ShapeDtypeStruct((HALF, 128), f32)),
        in_specs=[VMEM] * 6,
        out_specs=(HBM, VMEM),
        scratch_shapes=[pltpu.VMEM(step, jnp.bfloat16), pltpu.SemaphoreType.DMA((CHUNKS,))],
        compiler_params=SMALL,
        name="scaled_step",
    )(layers, hot, own, other, own_update, master)


def on_device(grads, memory, block_ids, layer_ids, master, first_moment, second_moment):
    block_ids, layer_ids = in_hbm(block_ids), in_hbm(layer_ids)
    master, first, second = master.T, first_moment.T, second_moment.T
    send, g_tiles, m_tiles = pack_send(block_ids, layer_ids, grads, memory)
    received = lax.ppermute(send, "dp", SWAP)
    keep, own, hot, layers = pack_keep(block_ids, layer_ids, g_tiles, m_tiles, master, first, second)
    part = (keep + received).reshape(YX, 64, 128)
    new_memory, done = filter_memory(block_ids, layer_ids, grads, memory, part)
    got = lax.all_to_all(part, "dp", 0, 0, axis_index_groups=YX_GROUPS, tiled=True)
    sums = partial_sums(got, own, done)
    got = lax.all_to_all(sums, "dp", 0, 0, axis_index_groups=Z_GROUPS, tiled=True)
    payload, own_sum, own_update = updates(got)
    mine = lax.all_to_all(payload, "dp", 0, 0, axis_index_groups=YX_GROUPS, tiled=True)
    other = lax.ppermute(mine, "dp", SWAP)
    first_new, second_new = new_moments(hot, own_sum, first, second)
    step_blocks, master_new = steps(layers, hot, mine, other, own_update, master)
    return (new_memory, master_new.T, first_new.T, second_new.T, step_blocks)


def solution(mesh):
    replica = P("dp", None, None)
    state = P(None, "dp")
    return jax.shard_map(
        on_device,
        mesh=mesh,
        in_specs=(replica, replica, P(), P(), state, state, state),
        out_specs=(replica, state, state, state, P()),
        check_vma=False,
    )
```

```python
import functools

import jax
import jax.numpy as jnp
from jax import lax
from jax.experimental import pallas as pl
from jax.experimental.pallas import tpu as pltpu
from jax.sharding import PartitionSpec as P

TILE = 128
SEL = 16
HALF = 64
Y, Z, X, C = 4, 8, 4, 2
YX = Y * X
TILES_SIDE = 8
BLOCKS_LAYER = 64

filter_rate = 0.3
beta_one = 0.9
beta_two = 0.999
adam_eps = 1e-06
weight_decay = 0.01
learn_rate = 0.01
norm_eps = 1e-06


def device(y, z, x, c):
    return ((y * Z + z) * X + x) * C + c


Z_ORDER = tuple(reversed(range(Z)))
YX_ORDER = tuple((y, x) for y in reversed(range(Y)) for x in reversed(range(X)))
Z_GROUPS = [[device(y, z, x, c) for z in Z_ORDER] for y in range(Y) for x in range(X) for c in range(C)]
YX_GROUPS = [[device(y, z, x, c) for y, x in YX_ORDER] for z in range(Z) for c in range(C)]
SWAP = [(i, i ^ 1) for i in range(Y * Z * X * C)]

f32 = jnp.float32
VMEM = pl.BlockSpec(memory_space=pltpu.VMEM)
SMEM = pl.BlockSpec(memory_space=pltpu.SMEM)
HBM = pl.BlockSpec(memory_space=pl.ANY)
LARGE = pltpu.CompilerParams(vmem_limit_bytes=16 << 20)
SMALL = pltpu.CompilerParams(vmem_limit_bytes=8 << 20)


def in_hbm(array):
    return pltpu.with_memory_space_constraint(array, pltpu.HBM)


def iota(shape, dim):
    return lax.broadcasted_iota(jnp.int32, shape, dim)


def one_hot(block_ref, layer_ref):
    sub = iota((SEL, 128), 0)
    column = jnp.zeros((SEL, 128), jnp.int32)
    for k in range(SEL):
        column = jnp.where(sub == k, layer_ref[k] * BLOCKS_LAYER + block_ref[k], column)
    return (column == iota((SEL, 128), 1)).astype(f32)


def layer_tile(layer_ref):
    sub = iota((8, 128), 0)
    low = iota((8, 128), 1) < HALF
    layer = jnp.zeros((8, 128), jnp.int32)
    for k in range(8):
        layer = jnp.where(sub == k, jnp.where(low, layer_ref[k], layer_ref[k + 8]), layer)
    return layer


def select_entries(hot, state):
    picked = lax.dot_general(
        hot, state, (((1,), (1,)), ((), ())), precision=lax.Precision.HIGHEST, preferred_element_type=f32
    )
    return jnp.concatenate([picked[:8], picked[8:]], axis=1)


def spread_entries(hot, tile):
    rows = jnp.concatenate([tile[:, :HALF], tile[:, HALF:]], axis=0)
    return lax.dot_general(
        rows, hot, (((0,), (0,)), ((), ())), precision=lax.Precision.HIGHEST, preferred_element_type=f32
    )


def half_columns(g_tiles, m_tiles, j, left):
    low = iota((TILE, TILE), 1) < HALF
    a = g_tiles[j].astype(f32) + m_tiles[j].astype(f32)
    b = g_tiles[j + 8].astype(f32) + m_tiles[j + 8].astype(f32)
    turned = pltpu.roll(jnp.where(left, b, a), HALF, 1)
    return jnp.where(low, jnp.where(left, a, turned), jnp.where(left, turned, b))


def store_rows(out_ref, tmp, j, value):
    tmp[j, pl.ds(0, TILE), :] = value
    for y in range(Y):
        for x in range(X):
            out_ref[pl.ds(YX_ORDER.index((y, x)) * 64 + j * 8, 8), :] = tmp[j, pl.ds(y * Z * X + x, Z, stride=X), :]


def send_kernel(block_ref, layer_ref, grads, memory, send_ref, g_tiles, m_tiles, tmp, g_sem, m_sem):
    copies = []
    for k in (j + 8 * h for j in range(8) for h in range(2)):
        layer = layer_ref[k]
        row = pl.multiple_of((block_ref[k] // TILES_SIDE) * TILE, TILE)
        col = pl.multiple_of((block_ref[k] % TILES_SIDE) * TILE, TILE)
        at = (layer, pl.ds(row, TILE), pl.ds(col, TILE))
        for src, buf, sem in ((grads, g_tiles, g_sem), (memory, m_tiles, m_sem)):
            copy = pltpu.make_async_copy(src.at[at], buf.at[k], sem.at[k])
            copy.start()
            copies.append(copy)
    for j in range(8):
        for copy in copies[4 * j : 4 * j + 4]:
            copy.wait()
        store_rows(send_ref, tmp, j, half_columns(g_tiles, m_tiles, j, lax.axis_index("dp") % C == 1))


def keep_kernel(block_ref, layer_ref, g_tiles, m_tiles, master, first, second, keep_ref, own_ref, hot_ref, layers_ref, tmp):
    for j in range(8):
        store_rows(keep_ref, tmp, j, half_columns(g_tiles, m_tiles, j, lax.axis_index("dp") % C == 0))
    hot = one_hot(block_ref, layer_ref)
    hot_ref[...] = hot
    layers_ref[...] = layer_tile(layer_ref)
    for i, state in enumerate((first, second, master)):
        own_ref[pl.ds(8 * i, 8), :] = select_entries(hot, state[...])


def pack_send(block_ids, layer_ids, grads, memory):
    tiles = jax.ShapeDtypeStruct((SEL, TILE, TILE), jnp.bfloat16)
    return pl.pallas_call(
        send_kernel,
        out_shape=(jax.ShapeDtypeStruct((1024, 128), f32), tiles, tiles),
        in_specs=[SMEM, SMEM, HBM, HBM],
        out_specs=(VMEM, VMEM, VMEM),
        scratch_shapes=[
            pltpu.VMEM((8, TILE + 8, TILE), f32),
            pltpu.SemaphoreType.DMA((SEL,)),
            pltpu.SemaphoreType.DMA((SEL,)),
        ],
        compiler_params=SMALL,
        name="pack_send",
    )(block_ids, layer_ids, in_hbm(grads), in_hbm(memory))


def pack_keep(block_ids, layer_ids, g_tiles, m_tiles, master, first, second):
    return pl.pallas_call(
        keep_kernel,
        out_shape=(
            jax.ShapeDtypeStruct((1024, 128), f32),
            jax.ShapeDtypeStruct((24, 128), f32),
            jax.ShapeDtypeStruct((SEL, 128), f32),
            jax.ShapeDtypeStruct((8, 128), jnp.int32),
        ),
        in_specs=[SMEM, SMEM, VMEM, VMEM, VMEM, VMEM, VMEM],
        out_specs=(VMEM, VMEM, VMEM, VMEM),
        scratch_shapes=[pltpu.VMEM((8, TILE + 8, TILE), f32)],
        compiler_params=SMALL,
        name="pack_keep",
    )(block_ids, layer_ids, g_tiles, m_tiles, master, first, second)


PARTS = 8
ROWS = 2 * 1024 // PARTS
CHUNK = 16


def filter_kernel(
    block_ref, layer_ref, grads, memory, after, out, done, g_buf, m_buf, o_buf, g_sem, m_sem, o_sem
):
    def rows(part):
        return pl.ds(pl.multiple_of(part * ROWS, ROWS), ROWS)

    def read(part, src, buf, sem):
        return pltpu.make_async_copy(src.at[rows(part)], buf.at[rows(part)], sem.at[part])

    def write(part):
        return pltpu.make_async_copy(o_buf.at[rows(part)], out.at[rows(part)], o_sem.at[part])

    @pl.loop(0, PARTS)
    def _(part):
        read(part, grads, g_buf, g_sem).start()
        read(part, memory, m_buf, m_sem).start()

    done[...] = jnp.zeros((8, 128), f32)
    tile = iota((8, 1024), 1) // TILE

    @pl.loop(0, PARTS)
    def _(part):
        read(part, grads, g_buf, g_sem).wait()
        read(part, memory, m_buf, m_sem).wait()
        for i in range(ROWS // TILE):
            column = tile + (part * (ROWS // TILE) + i) * TILES_SIDE
            chosen = jnp.zeros((8, 1024), jnp.bool_)
            for k in range(SEL):
                chosen = jnp.logical_or(chosen, column == layer_ref[k] * BLOCKS_LAYER + block_ref[k])
            rate = jnp.where(chosen, f32(0.0), f32(filter_rate))
            rate = jnp.concatenate([rate] * (CHUNK // 8), axis=0)

            @pl.loop(0, TILE // CHUNK, unroll=TILE // CHUNK)
            def _(c):
                at = pl.ds(pl.multiple_of(part * ROWS + i * TILE + c * CHUNK, CHUNK), CHUNK)
                mem = m_buf[at, :].astype(f32)
                total = g_buf[at, :].astype(f32) + mem
                mixed = f32(1.0 - filter_rate) * mem + rate * total
                o_buf[at, :] = mixed.astype(jnp.bfloat16)

        write(part).start()

    @pl.loop(0, PARTS)
    def _(part):
        write(part).wait()


def filter_memory(block_ids, layer_ids, grads, memory, after):
    flat = (2 * 1024, 1024)
    buf = pltpu.VMEM(flat, jnp.bfloat16)
    sem = pltpu.SemaphoreType.DMA((PARTS,))
    out, done = pl.pallas_call(
        filter_kernel,
        out_shape=(jax.ShapeDtypeStruct(flat, jnp.bfloat16), jax.ShapeDtypeStruct((8, 128), f32)),
        in_specs=[SMEM, SMEM, HBM, HBM, HBM],
        out_specs=(HBM, VMEM),
        scratch_shapes=[buf, buf, buf, sem, sem, sem],
        compiler_params=LARGE,
        cost_estimate=pl.CostEstimate(flops=8 << 20, bytes_accessed=12 << 20, transcendentals=0),
        name="filter_memory",
    )(block_ids, layer_ids, in_hbm(grads.reshape(flat)), in_hbm(memory.reshape(flat)), after)
    return out.reshape(2, 1024, 1024), done


def partial_kernel(got, own, out_ref, tmp, sem):
    for j in range(8):
        total = got[0, pl.ds(8 * j, 8), :]
        for s in range(1, YX):
            total = total + got[s, pl.ds(8 * j, 8), :]
        tmp[pl.ds(j, Z, stride=8), :] = total
    tmp[pl.ds(64, 24), :] = own[...]
    copies = [pltpu.make_async_copy(tmp.at[pl.ds(0, 88)], out_ref.at[z], sem.at[z]) for z in range(Z)]
    for copy in copies:
        copy.start()
    for copy in copies:
        copy.wait()


def partial_sums(got, own):
    return pl.pallas_call(
        partial_kernel,
        out_shape=jax.ShapeDtypeStruct((Z, 88, 128), f32),
        in_specs=[VMEM, VMEM],
        out_specs=HBM,
        scratch_shapes=[pltpu.VMEM((88, 128), f32), pltpu.SemaphoreType.DMA((Z,))],
        compiler_params=SMALL,
        name="sum_partials",
    )(got, own)


def update_kernel(got, after, out_ref, own_sum, own_update):
    me = lax.axis_index("dp") // (X * C) % Z
    squares = jnp.zeros((8, 128), f32)
    for z in range(Z):
        at = pl.ds(8 * z, 8)
        summed = got[0, at, :]
        for s in range(1, Z):
            summed = summed + got[s, at, :]
        first = got[Z_ORDER.index(z), pl.ds(64, 8), :]
        second = got[Z_ORDER.index(z), pl.ds(72, 8), :]
        weights = got[Z_ORDER.index(z), pl.ds(80, 8), :]
        first_sel = beta_one * first + (1.0 - beta_one) * summed
        second_sel = beta_two * second + (1.0 - beta_two) * summed * summed
        update = first_sel / (jnp.sqrt(second_sel) + adam_eps) + weight_decay * weights
        squares = squares + weights * weights
        for s in range(YX):
            out_ref[s, at, :] = update

        @pl.when(me == z)
        def _():
            own_sum[...] = summed
            own_update[...] = update

    for s in range(YX):
        out_ref[s, pl.ds(64, 8), :] = squares


def updates(got, after):
    tile = jax.ShapeDtypeStruct((8, 128), f32)
    return pl.pallas_call(
        update_kernel,
        out_shape=(jax.ShapeDtypeStruct((YX, 72, 128), f32), tile, tile),
        in_specs=[VMEM, VMEM],
        out_specs=(VMEM, VMEM, VMEM),
        compiler_params=SMALL,
        name="lamb_update",
    )(got, after)


def state_kernel(hot_ref, own_sum, first, second, first_new, second_new):
    hot = hot_ref[...]
    named = jnp.max(hot, axis=0, keepdims=True) > 0.5
    summed = spread_entries(hot, own_sum[...])
    old = first[...]
    first_new[...] = jnp.where(named, beta_one * old + (1.0 - beta_one) * summed, old)
    old = second[...]
    second_new[...] = jnp.where(named, beta_two * old + (1.0 - beta_two) * summed * summed, old)


def new_moments(hot, own_sum, first, second):
    state = jax.ShapeDtypeStruct((HALF, 128), f32)
    return pl.pallas_call(
        state_kernel,
        out_shape=(state, state),
        in_specs=[VMEM] * 4,
        out_specs=(VMEM, VMEM),
        compiler_params=SMALL,
        name="new_moments",
    )(hot, own_sum, first, second)


CHUNKS = 4
WIDTH = TILE * TILE // CHUNKS


def step_kernel(layers_ref, hot_ref, own, other, own_update, master, step_ref, master_new, buf, sem):
    update_sq = [jnp.zeros((8, 128), f32) for _ in range(4)]
    weight_sq = jnp.zeros((8, 128), f32)
    for ref in (own, other):
        for s in range(YX):
            for z in range(Z):
                value = ref[s, pl.ds(8 * z, 8), :]
                update_sq[z % 4] = update_sq[z % 4] + value * value
            weight_sq = weight_sq + ref[s, pl.ds(64, 8), :]
    update_sq = (update_sq[0] + update_sq[1]) + (update_sq[2] + update_sq[3])
    layer = layers_ref[...]
    ratio = jnp.zeros((8, 128), f32)
    for which in range(2):
        mine = layer == which
        weight_total = jnp.sum(jnp.where(mine, weight_sq, 0.0), keepdims=True)
        update_total = jnp.sum(jnp.where(mine, update_sq, 0.0), keepdims=True)
        ratio = jnp.where(mine, jnp.sqrt(weight_total / (update_total + norm_eps)), ratio)
    low = iota((8, 128), 1) < HALF
    first_core = lax.axis_index("dp") % C == 0

    def chunk(i):
        at = pl.ds(i * WIDTH, WIDTH)
        return pltpu.make_async_copy(buf.at[:, at], step_ref.at[:, at], sem.at[i])

    for y in range(Y):
        for z in range(Z):
            for x in range(X):
                at = (YX_ORDER.index((y, x)), pl.ds(8 * z, 8))
                a = ratio * own[at]
                b = ratio * other[at]
                turned = pltpu.roll(jnp.where(first_core, b, a), HALF, 1)
                straight = jnp.where(first_core, a, b)
                top = jnp.where(low, straight, turned)
                bottom = jnp.where(low, pltpu.roll(straight, HALF, 1), jnp.where(first_core, b, a))
                row = (y * Z + z) * X + x
                buf[:, pl.ds(row * TILE, TILE)] = jnp.concatenate([top, bottom], axis=0).astype(jnp.bfloat16)
        chunk(y).start()
    hot = hot_ref[...]
    named = jnp.max(hot, axis=0, keepdims=True) > 0.5
    scaled = spread_entries(hot, ratio * own_update[...])
    old = master[...]
    master_new[...] = jnp.where(named, old - learn_rate * scaled, old)
    for i in range(CHUNKS):
        chunk(i).wait()


def steps(layers, hot, own, other, own_update, master):
    step = (SEL, TILE * TILE)
    return pl.pallas_call(
        step_kernel,
        out_shape=(jax.ShapeDtypeStruct(step, jnp.bfloat16), jax.ShapeDtypeStruct((HALF, 128), f32)),
        in_specs=[VMEM] * 6,
        out_specs=(HBM, VMEM),
        scratch_shapes=[pltpu.VMEM(step, jnp.bfloat16), pltpu.SemaphoreType.DMA((CHUNKS,))],
        compiler_params=SMALL,
        name="scaled_step",
    )(layers, hot, own, other, own_update, master)


def on_device(grads, memory, block_ids, layer_ids, master, first_moment, second_moment):
    block_ids, layer_ids = in_hbm(block_ids), in_hbm(layer_ids)
    master, first, second = master.T, first_moment.T, second_moment.T
    send, g_tiles, m_tiles = pack_send(block_ids, layer_ids, grads, memory)
    received = lax.ppermute(send, "dp", SWAP)
    keep, own, hot, layers = pack_keep(block_ids, layer_ids, g_tiles, m_tiles, master, first, second)
    part = (keep + received).reshape(YX, 64, 128)
    got = lax.all_to_all(part, "dp", 0, 0, axis_index_groups=YX_GROUPS, tiled=True)
    sums = partial_sums(got, own)
    new_memory, done = filter_memory(block_ids, layer_ids, grads, memory, sums)
    got = lax.all_to_all(sums, "dp", 0, 0, axis_index_groups=Z_GROUPS, tiled=True)
    payload, own_sum, own_update = updates(got, done)
    mine = lax.all_to_all(payload, "dp", 0, 0, axis_index_groups=YX_GROUPS, tiled=True)
    other = lax.ppermute(mine, "dp", SWAP)
    first_new, second_new = new_moments(hot, own_sum, first, second)
    step_blocks, master_new = steps(layers, hot, mine, other, own_update, master)
    return (new_memory, master_new.T, first_new.T, second_new.T, step_blocks)


def solution(mesh):
    replica = P("dp", None, None)
    state = P(None, "dp")
    return jax.shard_map(
        on_device,
        mesh=mesh,
        in_specs=(replica, replica, P(), P(), state, state, state),
        out_specs=(replica, state, state, state, P()),
        check_vma=False,
    )
```

```python
import functools

import jax
import jax.numpy as jnp
from jax import lax
from jax.experimental import pallas as pl
from jax.experimental.pallas import tpu as pltpu
from jax.sharding import PartitionSpec as P

TILE = 128
SEL = 16
HALF = 64
Y, Z, X, C = 4, 8, 4, 2
YX = Y * X
TILES_SIDE = 8
BLOCKS_LAYER = 64

filter_rate = 0.3
beta_one = 0.9
beta_two = 0.999
adam_eps = 1e-06
weight_decay = 0.01
learn_rate = 0.01
norm_eps = 1e-06


def device(y, z, x, c):
    return ((y * Z + z) * X + x) * C + c


Z_ORDER = (7, 6, 5, 4, 3, 1, 2, 0)
YX_ORDER = tuple((y, x) for y in reversed(range(Y)) for x in reversed(range(X)))
Z_GROUPS = [[device(y, z, x, c) for z in Z_ORDER] for y in range(Y) for x in range(X) for c in range(C)]
YX_GROUPS = [[device(y, z, x, c) for y, x in YX_ORDER] for z in range(Z) for c in range(C)]
SWAP = [(i, i ^ 1) for i in range(Y * Z * X * C)]

f32 = jnp.float32
VMEM = pl.BlockSpec(memory_space=pltpu.VMEM)
SMEM = pl.BlockSpec(memory_space=pltpu.SMEM)
HBM = pl.BlockSpec(memory_space=pl.ANY)
LARGE = pltpu.CompilerParams(vmem_limit_bytes=16 << 20)
SMALL = pltpu.CompilerParams(vmem_limit_bytes=8 << 20)


def in_hbm(array):
    return pltpu.with_memory_space_constraint(array, pltpu.HBM)


def iota(shape, dim):
    return lax.broadcasted_iota(jnp.int32, shape, dim)


def one_hot(block_ref, layer_ref):
    sub = iota((SEL, 128), 0)
    column = jnp.zeros((SEL, 128), jnp.int32)
    for k in range(SEL):
        column = jnp.where(sub == k, layer_ref[k] * BLOCKS_LAYER + block_ref[k], column)
    return (column == iota((SEL, 128), 1)).astype(f32)


def layer_tile(layer_ref):
    sub = iota((8, 128), 0)
    low = iota((8, 128), 1) < HALF
    layer = jnp.zeros((8, 128), jnp.int32)
    for k in range(8):
        layer = jnp.where(sub == k, jnp.where(low, layer_ref[k], layer_ref[k + 8]), layer)
    return layer


def select_entries(hot, state):
    picked = lax.dot_general(
        hot, state, (((1,), (1,)), ((), ())), precision=lax.Precision.HIGHEST, preferred_element_type=f32
    )
    return jnp.concatenate([picked[:8], picked[8:]], axis=1)


def spread_entries(hot, tile):
    rows = jnp.concatenate([tile[:, :HALF], tile[:, HALF:]], axis=0)
    return lax.dot_general(
        rows, hot, (((0,), (0,)), ((), ())), precision=lax.Precision.HIGHEST, preferred_element_type=f32
    )


def half_columns(g_tiles, m_tiles, j, left):
    low = iota((TILE, TILE), 1) < HALF
    a = g_tiles[j].astype(f32) + m_tiles[j].astype(f32)
    b = g_tiles[j + 8].astype(f32) + m_tiles[j + 8].astype(f32)
    turned = pltpu.roll(jnp.where(left, b, a), HALF, 1)
    return jnp.where(low, jnp.where(left, a, turned), jnp.where(left, turned, b))


def store_rows(out_ref, tmp, j, value):
    tmp[j, pl.ds(0, TILE), :] = value
    for y in range(Y):
        for x in range(X):
            out_ref[pl.ds(YX_ORDER.index((y, x)) * 64 + j * 8, 8), :] = tmp[j, pl.ds(y * Z * X + x, Z, stride=X), :]


def send_kernel(block_ref, layer_ref, grads, memory, send_ref, g_tiles, m_tiles, tmp, g_sem, m_sem):
    copies = []
    for k in (j + 8 * h for j in range(8) for h in range(2)):
        layer = layer_ref[k]
        row = pl.multiple_of((block_ref[k] // TILES_SIDE) * TILE, TILE)
        col = pl.multiple_of((block_ref[k] % TILES_SIDE) * TILE, TILE)
        at = (layer, pl.ds(row, TILE), pl.ds(col, TILE))
        for src, buf, sem in ((grads, g_tiles, g_sem), (memory, m_tiles, m_sem)):
            copy = pltpu.make_async_copy(src.at[at], buf.at[k], sem.at[k])
            copy.start()
            copies.append(copy)
    for j in range(8):
        for copy in copies[4 * j : 4 * j + 4]:
            copy.wait()
        store_rows(send_ref, tmp, j, half_columns(g_tiles, m_tiles, j, lax.axis_index("dp") % C == 1))


def keep_kernel(block_ref, layer_ref, g_tiles, m_tiles, master, first, second, keep_ref, own_ref, hot_ref, layers_ref, tmp):
    for j in range(8):
        store_rows(keep_ref, tmp, j, half_columns(g_tiles, m_tiles, j, lax.axis_index("dp") % C == 0))
    hot = one_hot(block_ref, layer_ref)
    hot_ref[...] = hot
    layers_ref[...] = layer_tile(layer_ref)
    for i, state in enumerate((first, second, master)):
        own_ref[pl.ds(8 * i, 8), :] = select_entries(hot, state[...])


def pack_send(block_ids, layer_ids, grads, memory):
    tiles = jax.ShapeDtypeStruct((SEL, TILE, TILE), jnp.bfloat16)
    return pl.pallas_call(
        send_kernel,
        out_shape=(jax.ShapeDtypeStruct((1024, 128), f32), tiles, tiles),
        in_specs=[SMEM, SMEM, HBM, HBM],
        out_specs=(VMEM, VMEM, VMEM),
        scratch_shapes=[
            pltpu.VMEM((8, TILE + 8, TILE), f32),
            pltpu.SemaphoreType.DMA((SEL,)),
            pltpu.SemaphoreType.DMA((SEL,)),
        ],
        compiler_params=SMALL,
        name="pack_send",
    )(block_ids, layer_ids, in_hbm(grads), in_hbm(memory))


def pack_keep(block_ids, layer_ids, g_tiles, m_tiles, master, first, second):
    return pl.pallas_call(
        keep_kernel,
        out_shape=(
            jax.ShapeDtypeStruct((1024, 128), f32),
            jax.ShapeDtypeStruct((24, 128), f32),
            jax.ShapeDtypeStruct((SEL, 128), f32),
            jax.ShapeDtypeStruct((8, 128), jnp.int32),
        ),
        in_specs=[SMEM, SMEM, VMEM, VMEM, VMEM, VMEM, VMEM],
        out_specs=(VMEM, VMEM, VMEM, VMEM),
        scratch_shapes=[pltpu.VMEM((8, TILE + 8, TILE), f32)],
        compiler_params=SMALL,
        name="pack_keep",
    )(block_ids, layer_ids, g_tiles, m_tiles, master, first, second)


PARTS = 8
ROWS = 2 * 1024 // PARTS
CHUNK = 16


def filter_kernel(
    block_ref, layer_ref, grads, memory, after, out, done, g_buf, m_buf, o_buf, g_sem, m_sem, o_sem
):
    def rows(part):
        return pl.ds(pl.multiple_of(part * ROWS, ROWS), ROWS)

    def read(part, src, buf, sem):
        return pltpu.make_async_copy(src.at[rows(part)], buf.at[rows(part)], sem.at[part])

    def write(part):
        return pltpu.make_async_copy(o_buf.at[rows(part)], out.at[rows(part)], o_sem.at[part])

    @pl.loop(0, PARTS)
    def _(part):
        read(part, grads, g_buf, g_sem).start()
        read(part, memory, m_buf, m_sem).start()

    done[...] = jnp.zeros((8, 128), f32)
    tile = iota((8, 1024), 1) // TILE

    @pl.loop(0, PARTS)
    def _(part):
        read(part, grads, g_buf, g_sem).wait()
        read(part, memory, m_buf, m_sem).wait()
        for i in range(ROWS // TILE):
            column = tile + (part * (ROWS // TILE) + i) * TILES_SIDE
            chosen = jnp.zeros((8, 1024), jnp.bool_)
            for k in range(SEL):
                chosen = jnp.logical_or(chosen, column == layer_ref[k] * BLOCKS_LAYER + block_ref[k])
            rate = jnp.where(chosen, f32(0.0), f32(filter_rate))
            rate = jnp.concatenate([rate] * (CHUNK // 8), axis=0)

            @pl.loop(0, TILE // CHUNK, unroll=TILE // CHUNK)
            def _(c):
                at = pl.ds(pl.multiple_of(part * ROWS + i * TILE + c * CHUNK, CHUNK), CHUNK)
                mem = m_buf[at, :].astype(f32)
                total = g_buf[at, :].astype(f32) + mem
                mixed = f32(1.0 - filter_rate) * mem + rate * total
                o_buf[at, :] = mixed.astype(jnp.bfloat16)

        write(part).start()

    @pl.loop(0, PARTS)
    def _(part):
        write(part).wait()


def filter_memory(block_ids, layer_ids, grads, memory, after):
    flat = (2 * 1024, 1024)
    buf = pltpu.VMEM(flat, jnp.bfloat16)
    sem = pltpu.SemaphoreType.DMA((PARTS,))
    out, done = pl.pallas_call(
        filter_kernel,
        out_shape=(jax.ShapeDtypeStruct(flat, jnp.bfloat16), jax.ShapeDtypeStruct((8, 128), f32)),
        in_specs=[SMEM, SMEM, HBM, HBM, HBM],
        out_specs=(HBM, VMEM),
        scratch_shapes=[buf, buf, buf, sem, sem, sem],
        compiler_params=LARGE,
        cost_estimate=pl.CostEstimate(flops=8 << 20, bytes_accessed=12 << 20, transcendentals=0),
        name="filter_memory",
    )(block_ids, layer_ids, in_hbm(grads.reshape(flat)), in_hbm(memory.reshape(flat)), after)
    return out.reshape(2, 1024, 1024), done


def partial_kernel(got, own, out_ref, tmp, sem):
    for j in range(8):
        total = got[0, pl.ds(8 * j, 8), :]
        for s in range(1, YX):
            total = total + got[s, pl.ds(8 * j, 8), :]
        tmp[pl.ds(j, Z, stride=8), :] = total
    tmp[pl.ds(64, 24), :] = own[...]
    copies = [pltpu.make_async_copy(tmp.at[pl.ds(0, 88)], out_ref.at[z], sem.at[z]) for z in range(Z)]
    for copy in copies:
        copy.start()
    for copy in copies:
        copy.wait()


def partial_sums(got, own):
    return pl.pallas_call(
        partial_kernel,
        out_shape=jax.ShapeDtypeStruct((Z, 88, 128), f32),
        in_specs=[VMEM, VMEM],
        out_specs=HBM,
        scratch_shapes=[pltpu.VMEM((88, 128), f32), pltpu.SemaphoreType.DMA((Z,))],
        compiler_params=SMALL,
        name="sum_partials",
    )(got, own)


def update_kernel(got, after, out_ref, own_sum, own_update):
    me = lax.axis_index("dp") // (X * C) % Z
    squares = jnp.zeros((8, 128), f32)
    for z in range(Z):
        at = pl.ds(8 * z, 8)
        summed = got[0, at, :]
        for s in range(1, Z):
            summed = summed + got[s, at, :]
        first = got[Z_ORDER.index(z), pl.ds(64, 8), :]
        second = got[Z_ORDER.index(z), pl.ds(72, 8), :]
        weights = got[Z_ORDER.index(z), pl.ds(80, 8), :]
        first_sel = beta_one * first + (1.0 - beta_one) * summed
        second_sel = beta_two * second + (1.0 - beta_two) * summed * summed
        update = first_sel / (jnp.sqrt(second_sel) + adam_eps) + weight_decay * weights
        squares = squares + weights * weights
        for s in range(YX):
            out_ref[s, at, :] = update

        @pl.when(me == z)
        def _():
            own_sum[...] = summed
            own_update[...] = update

    for s in range(YX):
        out_ref[s, pl.ds(64, 8), :] = squares


def updates(got, after):
    tile = jax.ShapeDtypeStruct((8, 128), f32)
    return pl.pallas_call(
        update_kernel,
        out_shape=(jax.ShapeDtypeStruct((YX, 72, 128), f32), tile, tile),
        in_specs=[VMEM, VMEM],
        out_specs=(VMEM, VMEM, VMEM),
        compiler_params=SMALL,
        name="lamb_update",
    )(got, after)


def state_kernel(hot_ref, own_sum, first, second, first_new, second_new):
    hot = hot_ref[...]
    named = jnp.max(hot, axis=0, keepdims=True) > 0.5
    summed = spread_entries(hot, own_sum[...])
    old = first[...]
    first_new[...] = jnp.where(named, beta_one * old + (1.0 - beta_one) * summed, old)
    old = second[...]
    second_new[...] = jnp.where(named, beta_two * old + (1.0 - beta_two) * summed * summed, old)


def new_moments(hot, own_sum, first, second):
    state = jax.ShapeDtypeStruct((HALF, 128), f32)
    return pl.pallas_call(
        state_kernel,
        out_shape=(state, state),
        in_specs=[VMEM] * 4,
        out_specs=(VMEM, VMEM),
        compiler_params=SMALL,
        name="new_moments",
    )(hot, own_sum, first, second)


CHUNKS = 4
WIDTH = TILE * TILE // CHUNKS


def step_kernel(layers_ref, hot_ref, own, other, own_update, master, step_ref, master_new, buf, sem):
    update_sq = [jnp.zeros((8, 128), f32) for _ in range(4)]
    weight_sq = jnp.zeros((8, 128), f32)
    for ref in (own, other):
        for s in range(YX):
            for z in range(Z):
                value = ref[s, pl.ds(8 * z, 8), :]
                update_sq[z % 4] = update_sq[z % 4] + value * value
            weight_sq = weight_sq + ref[s, pl.ds(64, 8), :]
    update_sq = (update_sq[0] + update_sq[1]) + (update_sq[2] + update_sq[3])
    layer = layers_ref[...]
    ratio = jnp.zeros((8, 128), f32)
    for which in range(2):
        mine = layer == which
        weight_total = jnp.sum(jnp.where(mine, weight_sq, 0.0), keepdims=True)
        update_total = jnp.sum(jnp.where(mine, update_sq, 0.0), keepdims=True)
        ratio = jnp.where(mine, jnp.sqrt(weight_total / (update_total + norm_eps)), ratio)
    low = iota((8, 128), 1) < HALF
    first_core = lax.axis_index("dp") % C == 0

    def chunk(i):
        at = pl.ds(i * WIDTH, WIDTH)
        return pltpu.make_async_copy(buf.at[:, at], step_ref.at[:, at], sem.at[i])

    for y in range(Y):
        for z in range(Z):
            for x in range(X):
                at = (YX_ORDER.index((y, x)), pl.ds(8 * z, 8))
                a = ratio * own[at]
                b = ratio * other[at]
                turned = pltpu.roll(jnp.where(first_core, b, a), HALF, 1)
                straight = jnp.where(first_core, a, b)
                top = jnp.where(low, straight, turned)
                bottom = jnp.where(low, pltpu.roll(straight, HALF, 1), jnp.where(first_core, b, a))
                row = (y * Z + z) * X + x
                buf[:, pl.ds(row * TILE, TILE)] = jnp.concatenate([top, bottom], axis=0).astype(jnp.bfloat16)
        chunk(y).start()
    hot = hot_ref[...]
    named = jnp.max(hot, axis=0, keepdims=True) > 0.5
    scaled = spread_entries(hot, ratio * own_update[...])
    old = master[...]
    master_new[...] = jnp.where(named, old - learn_rate * scaled, old)
    for i in range(CHUNKS):
        chunk(i).wait()


def steps(layers, hot, own, other, own_update, master):
    step = (SEL, TILE * TILE)
    return pl.pallas_call(
        step_kernel,
        out_shape=(jax.ShapeDtypeStruct(step, jnp.bfloat16), jax.ShapeDtypeStruct((HALF, 128), f32)),
        in_specs=[VMEM] * 6,
        out_specs=(HBM, VMEM),
        scratch_shapes=[pltpu.VMEM(step, jnp.bfloat16), pltpu.SemaphoreType.DMA((CHUNKS,))],
        compiler_params=SMALL,
        name="scaled_step",
    )(layers, hot, own, other, own_update, master)


def on_device(grads, memory, block_ids, layer_ids, master, first_moment, second_moment):
    block_ids, layer_ids = in_hbm(block_ids), in_hbm(layer_ids)
    master, first, second = master.T, first_moment.T, second_moment.T
    send, g_tiles, m_tiles = pack_send(block_ids, layer_ids, grads, memory)
    received = lax.ppermute(send, "dp", SWAP)
    keep, own, hot, layers = pack_keep(block_ids, layer_ids, g_tiles, m_tiles, master, first, second)
    part = (keep + received).reshape(YX, 64, 128)
    got = lax.all_to_all(part, "dp", 0, 0, axis_index_groups=YX_GROUPS, tiled=True)
    sums = partial_sums(got, own)
    new_memory, done = filter_memory(block_ids, layer_ids, grads, memory, sums)
    got = lax.all_to_all(sums, "dp", 0, 0, axis_index_groups=Z_GROUPS, tiled=True)
    payload, own_sum, own_update = updates(got, done)
    mine = lax.all_to_all(payload, "dp", 0, 0, axis_index_groups=YX_GROUPS, tiled=True)
    other = lax.ppermute(mine, "dp", SWAP)
    first_new, second_new = new_moments(hot, own_sum, first, second)
    step_blocks, master_new = steps(layers, hot, mine, other, own_update, master)
    return (new_memory, master_new.T, first_new.T, second_new.T, step_blocks)


def solution(mesh):
    replica = P("dp", None, None)
    state = P(None, "dp")
    return jax.shard_map(
        on_device,
        mesh=mesh,
        in_specs=(replica, replica, P(), P(), state, state, state),
        out_specs=(replica, state, state, state, P()),
        check_vma=False,
    )
```
